32 devices in a mesh: row: 2 (over x), col: 4 (over y, core), depth: 4 (over z).
Axes of the slice: x: 2, y: 2, z: 4, core: 2. Of those that a mesh axis runs over, the one named last changes fastest.
Arguments:
- activations: float32 [256, 8192], P(('col', 'depth'), 'row'), may hold values from -0.375 to 0.375
- grad_output: float32 [256, 16384], P('row', ('col', 'depth')), may hold values from -6 to 6
- up_weight: float32 [8192, 16384], P('row', ('col', 'depth')), may hold values from -0.0625 to 0.0625
Outputs:
- grad_input: float32 [256, 8192], P(('col', 'depth'), 'row')
- grad_weight: float32 [8192, 16384], P('row', ('col', 'depth'))
The draws below stay inside these ranges and needn't reach their ends.
All inputs are finite; a program needn't handle non-finite values.
Results may differ from the reference program's by a relative error of at most 0.000075.
Values sent between devices are 32-bit elements; how exact they have to be, the bound alone decides.
A program may use at most 128 MiB of HBM per device.

```python
import jax
import jax.numpy as jnp
from jax import lax

D = 8192
F = 16384
TOKENS = 256


def with_spikes(result, own_key, source, target, shards_of, factor):
    def block_of(position):
        return (jnp.arange(result.shape[position]) // (result.shape[position] // shards_of)).reshape((-1,) + (1,) * (result.ndim - 1 - position))

    near = jax.random.permutation(own_key, shards_of)[block_of(target)]
    second = (block_of(target) + shards_of // 2) % shards_of
    return jnp.where((block_of(source) == near) | (block_of(source) == second), factor * result, result)


def block_scale(key, dims, cuts, low, high):
    gain, own = 1.0, jax.random.fold_in(key, 6)
    for axis_at, parts in cuts:
        steps = jnp.exp(jax.random.uniform(jax.random.fold_in(own, axis_at), (parts,), jnp.float32, low / len(cuts), high / len(cuts)))
        gain = gain * jnp.repeat(steps, dims[axis_at] // parts).reshape([-1 if axis == axis_at else 1 for axis in range(len(dims))])
    return gain


def bell_draw(key, extent, width, bound, cuts=(), dtype=jnp.bfloat16):
    values = jax.random.normal(key, extent, jnp.float32) * width
    if len(cuts) > 0:
        values = block_scale(key, extent, cuts, -0.22, 0.18) * values
    return jnp.clip(values, min=-bound, max=bound).astype(dtype)


def noise_with(stream_key, shape, spread, most, shards, heavy, held_as=jnp.bfloat16):
    result = spread * jax.random.normal(stream_key, shape, jnp.float32)
    if shards:
        result = result * block_scale(stream_key, shape, shards, -0.22, 0.18)
    return jnp.clip(with_spikes(result, jax.random.fold_in(stream_key, 3), *heavy), -most, most).astype(held_as)


def setup_inputs(seed: int = 0) -> dict:
    keys = jax.random.split(jax.random.key(seed), 4)
    return {
        "activations": bell_draw(keys[0], (TOKENS, D), (TOKENS ** -0.5), 0.375, ((0, 16), (1, 2)), jnp.float32),
        "grad_output": noise_with(keys[1], (TOKENS, F), 1.0, 6.0, ((0, 2), (1, 16)), (1, 0, 16, 2.0), jnp.float32),
        "up_weight": bell_draw(keys[2], (D, F), D ** -0.5, 0.0625, ((0, 2), (1, 16)), jnp.float32),
    }


def reference(activations, grad_output, up_weight):
    highest = lax.Precision.HIGHEST
    grad_input = jnp.dot(grad_output, up_weight.T, precision=highest, preferred_element_type=jnp.float32)
    grad_weight = jnp.dot(activations.T, grad_output, precision=highest, preferred_element_type=jnp.float32)
    return grad_input, grad_weight
```

```python
import functools

import jax
import jax.numpy as jnp
from jax import lax
from jax.experimental import pallas as pl
from jax.experimental.pallas import tpu as pltpu
from jax.sharding import PartitionSpec as P

MESH = pl.DeviceIdType.MESH
NY = 2
UP, DOWN, ACROSS, PAIR = range(4)


def both(a, b):
    return jnp.logical_and(a, b)


def split(value):
    high = value.astype(jnp.bfloat16)
    low = (value - high.astype(jnp.float32)).astype(jnp.bfloat16)
    return high, low


def dot_nt(a, b):
    return lax.dot_general(
        a, b, (((1,), (1,)), ((), ())), preferred_element_type=jnp.float32
    )


def exchange_kernel(
    rows, nd, cuts, tile,
    acts_ref, grads_ref, weight_ref,
    out_ref, ath_ref, atl_ref, gh_ref, gl_ref,
    acts, grads, stage, wh, wl, part, rc, ry_a, ry_b, rz_a, rz_b,
    w_sem, x_s, x_r, ag_s, ag_r, c_s, c_r, ya_s, ya_r, yb_s, yb_r, za_s, za_r, zb_s, zb_r,
):
    x = lax.axis_index("row")
    col = lax.axis_index("col")
    z = lax.axis_index("depth")
    y, c = col // 2, col % 2
    oy, oc = 1 - y, 1 - c
    y1 = x * NY // rows
    tb, dm = acts_ref.shape
    trow = grads_ref.shape[0]
    tiles = dm // tile
    per = rows // NY
    has_up, has_down = z < nd - 1, z > 0

    mate = {"col": 2 * y + oc}
    across = {"col": 2 * oy + c}
    above, below = {"depth": z + 1}, {"depth": z - 1}

    def blk(yy, cc, zz):
        return (2 * yy + cc) * nd + zz

    me = blk(y, c, z)
    started = []

    def send(cond, make):
        def go():
            make().start()

        started.append((cond, make))
        if cond is None:
            go()
        else:
            pl.when(cond)(go)

    def weight_copy(i, slot):
        return pltpu.make_async_copy(
            weight_ref.at[pl.ds(i * tile, tile), :], stage.at[slot], w_sem.at[slot]
        )

    slots = min(3, tiles)
    for i in range(slots):
        weight_copy(i, i).start()

    acts[me] = acts_ref[...]
    grads[x] = grads_ref[...]

    barrier = pltpu.get_barrier_semaphore()
    peers = [{"row": (x + d) % rows} for d in range(1, rows)]
    for peer in [mate, across] + peers:
        pl.semaphore_signal(barrier, inc=1, device_id=peer, device_id_type=MESH)

    @pl.when(has_up)
    def _():
        pl.semaphore_signal(barrier, inc=1, device_id=above, device_id_type=MESH)

    @pl.when(has_down)
    def _():
        pl.semaphore_signal(barrier, inc=1, device_id=below, device_id_type=MESH)

    lines = has_up.astype(jnp.int32) + has_down.astype(jnp.int32)
    pl.semaphore_wait(barrier, 2 + len(peers) + lines)

    def x_copy(d):
        return pltpu.make_async_remote_copy(
            src_ref=grads.at[x], dst_ref=grads.at[x],
            send_sem=x_s.at[d], recv_sem=x_r.at[x],
            device_id={"row": (x + d) % rows}, device_id_type=MESH,
        )

    for d in range(1, rows):
        send(None, functools.partial(x_copy, d))

    targets = {UP: above, DOWN: below, ACROSS: across, PAIR: mate}

    def ag_copy(p, b, way):
        ref = acts.at[b, :, pl.ds(cuts[p], cuts[p + 1] - cuts[p])]
        return pltpu.make_async_remote_copy(
            src_ref=ref, dst_ref=ref,
            send_sem=ag_s.at[p, b, way], recv_sem=ag_r.at[p, b],
            device_id=targets[way], device_id_type=MESH,
        )

    def ag_send(cond, p, b, way):
        send(cond, lambda: ag_copy(p, b, way))

    def ag_wait(cond, p, b):
        def go():
            ag_copy(p, b, PAIR).wait_recv()

        if cond is None:
            go()
        else:
            pl.when(cond)(go)

    for p in range(2):
        ag_send(has_up, p, me, UP)
        ag_send(has_down, p, me, DOWN)
    ag_send(None, 1, me, ACROSS)
    ag_send(None, 0, me, ACROSS)
    for p in range(2):
        ag_send(None, p, me, PAIR)

    def ag_line(p, yy, s):
        low, high = z - s >= 0, z + s <= nd - 1
        b_low, b_high = blk(yy, c, z - s), blk(yy, c, z + s)
        ag_wait(low, p, b_low)
        ag_send(both(low, has_up), p, b_low, UP)
        if p == 0:
            ag_send(low, p, b_low, ACROSS)
        ag_send(low, p, b_low, PAIR)
        ag_wait(high, p, b_high)
        ag_send(both(high, has_down), p, b_high, DOWN)
        if p == 0:
            ag_send(high, p, b_high, ACROSS)
        ag_send(high, p, b_high, PAIR)

    def ag_cross(p, s):
        if s == 0:
            b = blk(oy, c, z)
            ag_wait(None, p, b)
            if p == 1:
                ag_send(has_up, p, b, UP)
                ag_send(has_down, p, b, DOWN)
            ag_send(None, p, b, PAIR)
        elif p == 1:
            ag_line(1, oy, s)
        else:
            for cond, b in (
                (z - s >= 0, blk(oy, c, z - s)),
                (z + s <= nd - 1, blk(oy, c, z + s)),
            ):
                ag_wait(cond, 0, b)
                ag_send(cond, 0, b, PAIR)

    def partial(phase):
        yy = (y1 + phase) % NY
        for j in range(per):
            q = yy * per + j

            @pl.when(q != x)
            def _():
                pltpu.make_async_remote_copy(
                    src_ref=grads.at[q], dst_ref=grads.at[q],
                    send_sem=x_s.at[0], recv_sem=x_r.at[q],
                    device_id=mate, device_id_type=MESH,
                ).wait_recv()

            high, low = split(grads[q])
            at = pl.ds(pl.multiple_of(q * trow, trow), trow)
            gh_ref[at, :] = high
            gl_ref[at, :] = low
        half = per * trow
        at = pl.ds(pl.multiple_of(yy * half, half), half)

        def step(i, carry):
            rows_at = pl.ds(pl.multiple_of(i * tile, tile), tile)
            if phase == 0:
                slot = i % slots
                weight_copy(i, slot).wait()
                high, low = split(stage[slot])
                wh[rows_at, :] = high
                wl[rows_at, :] = low

                @pl.when(i + slots < tiles)
                def _():
                    weight_copy(i + slots, slot).start()
            else:
                high, low = wh[rows_at, :], wl[rows_at, :]
            g_high, g_low = gh_ref[at, :], gl_ref[at, :]
            total = dot_nt(g_high, high) + (dot_nt(g_low, high) + dot_nt(g_high, low))
            part[pl.ds(yy * 2 * nd, 2 * nd), :, rows_at] = total.reshape(
                2 * nd, tb, tile
            )
            return carry

        lax.fori_loop(0, tiles, step, 0)

    def cols(p):
        return pl.ds(cuts[p], cuts[p + 1] - cuts[p])

    def pair_copy(yy, p):
        return pltpu.make_async_remote_copy(
            src_ref=part.at[pl.ds(blk(yy, oc, 0), nd), :, cols(p)],
            dst_ref=rc.at[yy, :, :, cols(p)],
            send_sem=c_s.at[yy, p], recv_sem=c_r.at[yy, p],
            device_id=mate, device_id_type=MESH,
        )

    def pair_send(phase):
        yy = (y1 + phase) % NY
        for p in range(2):
            send(None, functools.partial(pair_copy, yy, p))

    def pair_add(phase, p):
        yy = (y1 + phase) % NY
        pair_copy(yy, p).wait_recv()
        own = pl.ds(blk(yy, c, 0), nd)
        part[own, :, cols(p)] += rc[yy, :, :, cols(p)]

    def across_copy(t):
        return pltpu.make_async_remote_copy(
            src_ref=part.at[blk(oy, c, t), :, cols(0)], dst_ref=ry_a.at[t],
            send_sem=ya_s.at[t], recv_sem=ya_r.at[t],
            device_id=across, device_id_type=MESH,
        )

    def across_send(phase):
        yy = (y1 + phase) % NY
        order = sorted(range(nd), key=lambda t: -abs(2 * t - nd + 1))
        for t in order:
            send(yy != y, functools.partial(across_copy, t))

    def across_add():
        order = sorted(range(nd), key=lambda t: -abs(2 * t - nd + 1))
        for t in order:
            across_copy(t).wait_recv()
            part[blk(y, c, t), :, cols(0)] += ry_a[t]

    def line_copy(p, yy, t, way):
        if p == 0:
            dst, ss, rs = rz_a.at[way, t], za_s.at[way, t], za_r.at[way, t]
        else:
            dst, ss, rs = rz_b.at[yy, way, t], zb_s.at[yy, way, t], zb_r.at[yy, way, t]
        return pltpu.make_async_remote_copy(
            src_ref=part.at[blk(yy, c, t), :, cols(p)], dst_ref=dst,
            send_sem=ss, recv_sem=rs,
            device_id=targets[way], device_id_type=MESH,
        )

    def line_take(p, yy, t, way):
        line_copy(p, yy, t, way).wait_recv()
        got = rz_a[way, t] if p == 0 else rz_b[yy, way, t]
        part[blk(yy, c, t), :, cols(p)] += got

    def line_step(p, yy, s, cond=None):
        for t, way, mine, more in (
            (nd - 1 - s, UP, z < nd - 1 - s, has_down),
            (s, DOWN, z > s, has_up),
        ):
            on = mine if cond is None else both(cond, mine)
            pl.when(both(on, more))(functools.partial(line_take, p, yy, t, way))
            send(on, functools.partial(line_copy, p, yy, t, way))

    def line_end(p, yy, cond=None):
        for way, more in ((UP, has_down), (DOWN, has_up)):
            on = more if cond is None else both(cond, more)
            pl.when(on)(functools.partial(line_take, p, yy, z, way))

    def last_copy():
        return pltpu.make_async_remote_copy(
            src_ref=part.at[blk(oy, c, z), :, cols(1)], dst_ref=ry_b,
            send_sem=yb_s, recv_sem=yb_r,
            device_id=across, device_id_type=MESH,
        )

    y2 = (y1 + 1) % NY
    first, second = y == y1, y != y1

    partial(0)
    pair_send(0)
    ag_cross(1, 0)
    ag_line(0, y, 1)
    ag_line(1, y, 1)
    pair_add(0, 0)
    across_send(0)
    pair_add(0, 1)
    line_step(1, y1, 0)
    ag_cross(0, 0)
    ag_cross(1, 1)
    ag_line(0, y, 2)
    ag_line(1, y, 2)
    partial(1)
    pair_send(1)
    line_step(1, y1, 1)
    pair_add(1, 0)
    across_send(1)
    pair_add(1, 1)
    line_step(1, y2, 0)
    for s in range(3, nd):
        ag_line(0, y, s)
        ag_line(1, y, s)
    for s in range(2, nd):
        ag_cross(1, s)
    pl.when(first)(across_add)
    line_step(0, y, 0, first)
    for s in range(2, nd - 1):
        line_step(1, y1, s)
    line_step(0, y, 1, first)
    line_step(1, y2, 1)
    line_end(1, y1)
    send(second, last_copy)
    pl.when(second)(across_add)
    line_step(0, y, 0, second)
    for s in range(2, nd - 1):
        line_step(0, y, s, first)
    for s in range(2, nd - 1):
        line_step(1, y2, s)
    line_step(0, y, 1, second)
    line_end(1, y2)
    send(first, last_copy)
    for s in range(2, nd - 1):
        line_step(0, y, s, second)

    for s in range(1, nd):
        ag_cross(0, s)
    for p in range(2):
        for yy in range(NY):
            for zz in range(nd):
                ag_wait(None, p, blk(yy, oc, zz))

    def turn(i, carry):
        at = pl.ds(pl.multiple_of(i * tile, tile), tile)
        block = acts[:, :, at].reshape(2 * NY * nd * tb, tile)
        high, low = split(block.T)
        ath_ref[at, :] = high
        atl_ref[at, :] = low
        return carry

    lax.fori_loop(0, tiles, turn, 0)

    line_end(0, y)
    last_copy().wait_recv()
    part[me, :, cols(1)] += ry_b[...]
    out_ref[...] = part[me]

    for cond, make in started:
        if cond is None:
            make().wait_send()
        else:
            pl.when(cond)(lambda make=make: make().wait_send())


def weight_kernel(ath_ref, atl_ref, gh_ref, gl_ref, out_ref):
    def dot(a, b):
        return jnp.dot(a, b, preferred_element_type=jnp.float32)

    high = ath_ref[...]
    out_ref[...] = dot(high, gh_ref[...]) + (
        dot(high, gl_ref[...]) + dot(atl_ref[...], gh_ref[...])
    )


def shards(rows, nc, nd, activations, grad_output, up_weight):
    tb, dm = activations.shape
    trow, df = grad_output.shape
    tokens = trow * rows
    tile = min(512, dm)
    f32, bf16 = jnp.float32, jnp.bfloat16
    step = max(128, dm // 8)
    cuts = (0, (dm // step * 5 // 8) * step, dm)
    wa, wb = cuts[1], dm - cuts[1]
    vmem = pl.BlockSpec(memory_space=pltpu.VMEM)
    dma = pltpu.SemaphoreType.DMA
    grad_input, ath, atl, gh, gl = pl.pallas_call(
        functools.partial(exchange_kernel, rows, nd, cuts, tile),
        out_shape=(
            jax.ShapeDtypeStruct((tb, dm), f32),
            jax.ShapeDtypeStruct((dm, tokens), bf16),
            jax.ShapeDtypeStruct((dm, tokens), bf16),
            jax.ShapeDtypeStruct((tokens, df), bf16),
            jax.ShapeDtypeStruct((tokens, df), bf16),
        ),
        in_specs=[vmem, vmem, pl.BlockSpec(memory_space=pl.ANY)],
        out_specs=(vmem,) * 5,
        scratch_shapes=[
            pltpu.VMEM((nc * nd, tb, dm), f32),
            pltpu.VMEM((rows, trow, df), f32),
            pltpu.VMEM((min(3, dm // tile), tile, df), f32),
            pltpu.VMEM((dm, df), bf16),
            pltpu.VMEM((dm, df), bf16),
            pltpu.VMEM((nc * nd, tb, dm), f32),
            pltpu.VMEM((NY, nd, tb, dm), f32),
            pltpu.VMEM((nd, tb, wa), f32),
            pltpu.VMEM((tb, wb), f32),
            pltpu.VMEM((2, nd, tb, wa), f32),
            pltpu.VMEM((NY, 2, nd, tb, wb), f32),
            dma((3,)),
            dma((rows,)),
            dma((rows,)),
            dma((2, nc * nd, 4)),
            dma((2, nc * nd)),
            dma((NY, 2)),
            dma((NY, 2)),
            dma((nd,)),
            dma((nd,)),
            dma,
            dma,
            dma((2, nd)),
            dma((2, nd)),
            dma((NY, 2, nd)),
            dma((NY, 2, nd)),
        ],
        compiler_params=pltpu.CompilerParams(
            collective_id=0, has_side_effects=True, vmem_limit_bytes=60 * 2**20
        ),
        cost_estimate=pl.CostEstimate(
            flops=6 * tokens * dm * df, bytes_accessed=4 * dm * df, transcendentals=0
        ),
        name="exchange",
    )(activations, grad_output, up_weight)

    grad_weight = pl.pallas_call(
        weight_kernel,
        grid=(dm // tile,),
        out_shape=jax.ShapeDtypeStruct((dm, df), f32),
        in_specs=[
            pl.BlockSpec((tile, tokens), lambda i: (i, 0)),
            pl.BlockSpec((tile, tokens), lambda i: (i, 0)),
            pl.BlockSpec((tokens, df), lambda i: (0, 0)),
            pl.BlockSpec((tokens, df), lambda i: (0, 0)),
        ],
        out_specs=pl.BlockSpec((tile, df), lambda i: (i, 0)),
        compiler_params=pltpu.CompilerParams(vmem_limit_bytes=48 * 2**20),
        cost_estimate=pl.CostEstimate(
            flops=6 * tokens * dm * df, bytes_accessed=4 * dm * df, transcendentals=0
        ),
        name="weight_grad",
    )(ath, atl, gh, gl)
    return grad_input, grad_weight


def solution(mesh):
    rows, nc, nd = (mesh.shape[name] for name in ("row", "col", "depth"))
    return jax.shard_map(
        functools.partial(shards, rows, nc, nd),
        mesh=mesh,
        in_specs=(
            P(("col", "depth"), "row"),
            P("row", ("col", "depth")),
            P("row", ("col", "depth")),
        ),
        out_specs=(P(("col", "depth"), "row"), P("row", ("col", "depth"))),
        check_vma=False,
    )
```

```python
import functools

import jax
import jax.numpy as jnp
from jax import lax
from jax.experimental import pallas as pl
from jax.experimental.pallas import tpu as pltpu
from jax.sharding import PartitionSpec as P

MESH = pl.DeviceIdType.MESH
NY = 2
UP, DOWN, ACROSS, PAIR = range(4)


def both(a, b):
    return jnp.logical_and(a, b)


def split(value):
    high = value.astype(jnp.bfloat16)
    low = (value - high.astype(jnp.float32)).astype(jnp.bfloat16)
    return high, low


def dot_nt(a, b):
    return lax.dot_general(
        a, b, (((1,), (1,)), ((), ())), preferred_element_type=jnp.float32
    )


def exchange_kernel(
    rows, nd, cuts, tile,
    acts_ref, grads_ref, weight_ref,
    out_ref, ath_ref, atl_ref, gh_ref, gl_ref,
    acts, grads, gcat, th, tl, stage, wh, wl, part, rc, ry_a, ry_b, rz_a, rz_b,
    t_sem, w_sem, x_s, x_r, ag_s, ag_r, c_s, c_r, ya_s, ya_r, yb_s, yb_r, za_s, za_r, zb_s, zb_r,
):
    x = lax.axis_index("row")
    col = lax.axis_index("col")
    z = lax.axis_index("depth")
    y, c = col // 2, col % 2
    oy, oc = 1 - y, 1 - c
    y1 = x * NY // rows
    tb, dm = acts_ref.shape
    trow = grads_ref.shape[0]
    tiles = dm // tile
    per = rows // NY
    has_up, has_down = z < nd - 1, z > 0

    mate = {"col": 2 * y + oc}
    across = {"col": 2 * oy + c}
    above, below = {"depth": z + 1}, {"depth": z - 1}

    def blk(yy, cc, zz):
        return (2 * yy + cc) * nd + zz

    me = blk(y, c, z)
    started = []

    def send(cond, make):
        def go():
            make().start()

        started.append((cond, make))
        if cond is None:
            go()
        else:
            pl.when(cond)(go)

    def weight_copy(i, slot):
        return pltpu.make_async_copy(
            weight_ref.at[pl.ds(i * tile, tile), :], stage.at[slot], w_sem.at[slot]
        )

    slots = min(3, tiles)
    for i in range(slots):
        weight_copy(i, i).start()

    acts[me] = acts_ref[...]
    grads[x] = grads_ref[...]

    barrier = pltpu.get_barrier_semaphore()
    peers = [{"row": (x + d) % rows} for d in range(1, rows)]
    for peer in [mate, across] + peers:
        pl.semaphore_signal(barrier, inc=1, device_id=peer, device_id_type=MESH)

    @pl.when(has_up)
    def _():
        pl.semaphore_signal(barrier, inc=1, device_id=above, device_id_type=MESH)

    @pl.when(has_down)
    def _():
        pl.semaphore_signal(barrier, inc=1, device_id=below, device_id_type=MESH)

    lines = has_up.astype(jnp.int32) + has_down.astype(jnp.int32)
    pl.semaphore_wait(barrier, 2 + len(peers) + lines)

    def x_copy(d):
        return pltpu.make_async_remote_copy(
            src_ref=grads.at[x], dst_ref=grads.at[x],
            send_sem=x_s.at[d], recv_sem=x_r.at[x],
            device_id={"row": (x + d) % rows}, device_id_type=MESH,
        )

    for d in range(1, rows):
        send(None, functools.partial(x_copy, d))

    targets = {UP: above, DOWN: below, ACROSS: across, PAIR: mate}

    def ag_copy(p, b, way):
        ref = acts.at[b, :, pl.ds(cuts[p], cuts[p + 1] - cuts[p])]
        return pltpu.make_async_remote_copy(
            src_ref=ref, dst_ref=ref,
            send_sem=ag_s.at[p, b, way], recv_sem=ag_r.at[p, b],
            device_id=targets[way], device_id_type=MESH,
        )

    def ag_send(cond, p, b, way):
        send(cond, lambda: ag_copy(p, b, way))

    def ag_wait(cond, p, b):
        def go():
            ag_copy(p, b, PAIR).wait_recv()

        if cond is None:
            go()
        else:
            pl.when(cond)(go)

    for p in range(2):
        ag_send(has_up, p, me, UP)
        ag_send(has_down, p, me, DOWN)
    ag_send(None, 1, me, ACROSS)
    ag_send(None, 0, me, ACROSS)
    for p in range(2):
        ag_send(None, p, me, PAIR)

    def ag_line(p, yy, s):
        low, high = z - s >= 0, z + s <= nd - 1
        b_low, b_high = blk(yy, c, z - s), blk(yy, c, z + s)
        ag_wait(low, p, b_low)
        ag_send(both(low, has_up), p, b_low, UP)
        if p == 0:
            ag_send(low, p, b_low, ACROSS)
        ag_send(low, p, b_low, PAIR)
        ag_wait(high, p, b_high)
        ag_send(both(high, has_down), p, b_high, DOWN)
        if p == 0:
            ag_send(high, p, b_high, ACROSS)
        ag_send(high, p, b_high, PAIR)

    def ag_cross(p, s):
        if s == 0:
            b = blk(oy, c, z)
            ag_wait(None, p, b)
            if p == 1:
                ag_send(has_up, p, b, UP)
                ag_send(has_down, p, b, DOWN)
            ag_send(None, p, b, PAIR)
        elif p == 1:
            ag_line(1, oy, s)
        else:
            for cond, b in (
                (z - s >= 0, blk(oy, c, z - s)),
                (z + s <= nd - 1, blk(oy, c, z + s)),
            ):
                ag_wait(cond, 0, b)
                ag_send(cond, 0, b, PAIR)

    half = per * trow

    def prepare(phase):
        yy = (y1 + phase) % NY
        for j in range(per):
            q = yy * per + j

            @pl.when(q != x)
            def _():
                pltpu.make_async_remote_copy(
                    src_ref=grads.at[q], dst_ref=grads.at[q],
                    send_sem=x_s.at[0], recv_sem=x_r.at[q],
                    device_id=mate, device_id_type=MESH,
                ).wait_recv()

            high, low = split(grads[q])
            at = pl.ds(pl.multiple_of(q * trow, trow), trow)
            gh_ref[at, :] = high
            gl_ref[at, :] = low
            gcat[phase, j * trow : (j + 1) * trow, :] = high
            gcat[phase, half + j * trow : half + (j + 1) * trow, :] = low

    def partial(phase, p):
        yy = (y1 + phase) % NY

        def step(i, carry):
            rows_at = pl.ds(pl.multiple_of(i * tile, tile), tile)
            if phase == 0:
                slot = i % slots
                weight_copy(i, slot).wait()
                high, low = split(stage[slot])
                wh[rows_at, :] = high
                wl[rows_at, :] = low

                @pl.when(i + slots < tiles)
                def _():
                    weight_copy(i + slots, slot).start()
            else:
                high, low = wh[rows_at, :], wl[rows_at, :]
            pairs = dot_nt(gcat[phase], high)
            total = pairs[:half] + (pairs[half:] + dot_nt(gcat[phase, :half, :], low))
            part[pl.ds(yy * 2 * nd, 2 * nd), :, rows_at] = total.reshape(
                2 * nd, tb, tile
            )
            return carry

        lax.fori_loop(cuts[p] // tile, cuts[p + 1] // tile, step, 0)

    def cols(p):
        return pl.ds(cuts[p], cuts[p + 1] - cuts[p])

    def pair_copy(yy, p):
        return pltpu.make_async_remote_copy(
            src_ref=part.at[pl.ds(blk(yy, oc, 0), nd), :, cols(p)],
            dst_ref=rc.at[yy, :, :, cols(p)],
            send_sem=c_s.at[yy, p], recv_sem=c_r.at[yy, p],
            device_id=mate, device_id_type=MESH,
        )

    def pair_send(phase, p):
        yy = (y1 + phase) % NY
        send(None, functools.partial(pair_copy, yy, p))

    def pair_add(phase, p):
        yy = (y1 + phase) % NY
        pair_copy(yy, p).wait_recv()
        own = pl.ds(blk(yy, c, 0), nd)
        part[own, :, cols(p)] += rc[yy, :, :, cols(p)]

    def across_copy(t):
        return pltpu.make_async_remote_copy(
            src_ref=part.at[blk(oy, c, t), :, cols(0)], dst_ref=ry_a.at[t],
            send_sem=ya_s.at[t], recv_sem=ya_r.at[t],
            device_id=across, device_id_type=MESH,
        )

    def across_send(phase):
        yy = (y1 + phase) % NY
        order = sorted(range(nd), key=lambda t: -abs(2 * t - nd + 1))
        for t in order:
            send(yy != y, functools.partial(across_copy, t))

    def across_add():
        order = sorted(range(nd), key=lambda t: -abs(2 * t - nd + 1))
        for t in order:
            across_copy(t).wait_recv()
            part[blk(y, c, t), :, cols(0)] += ry_a[t]

    def line_copy(p, yy, t, way):
        if p == 0:
            dst, ss, rs = rz_a.at[way, t], za_s.at[way, t], za_r.at[way, t]
        else:
            dst, ss, rs = rz_b.at[yy, way, t], zb_s.at[yy, way, t], zb_r.at[yy, way, t]
        return pltpu.make_async_remote_copy(
            src_ref=part.at[blk(yy, c, t), :, cols(p)], dst_ref=dst,
            send_sem=ss, recv_sem=rs,
            device_id=targets[way], device_id_type=MESH,
        )

    def line_take(p, yy, t, way):
        line_copy(p, yy, t, way).wait_recv()
        got = rz_a[way, t] if p == 0 else rz_b[yy, way, t]
        part[blk(yy, c, t), :, cols(p)] += got

    def line_edge(p, yy, cond=None):
        for on, way, order in (
            (z == 0, UP, range(nd - 1, 0, -1)),
            (z == nd - 1, DOWN, range(nd - 1)),
        ):
            on = on if cond is None else both(cond, on)
            for t in order:
                send(on, functools.partial(line_copy, p, yy, t, way))

    def line_step(p, yy, s, cond=None):
        for t, way, mine, more in (
            (nd - 1 - s, UP, z < nd - 1 - s, has_down),
            (s, DOWN, z > s, has_up),
        ):
            on = both(mine, more) if cond is None else both(cond, both(mine, more))
            pl.when(on)(functools.partial(line_take, p, yy, t, way))
            send(on, functools.partial(line_copy, p, yy, t, way))

    def line_end(p, yy, cond=None):
        for way, more in ((UP, has_down), (DOWN, has_up)):
            on = more if cond is None else both(cond, more)
            pl.when(on)(functools.partial(line_take, p, yy, z, way))

    def last_copy():
        return pltpu.make_async_remote_copy(
            src_ref=part.at[blk(oy, c, z), :, cols(1)], dst_ref=ry_b,
            send_sem=yb_s, recv_sem=yb_r,
            device_id=across, device_id_type=MESH,
        )

    y2 = (y1 + 1) % NY
    first, second = y == y1, y != y1

    prepare(0)
    for p in range(2):
        partial(0, p)
        pair_send(0, p)
    pair_add(0, 0)
    across_send(0)
    ag_cross(1, 0)
    ag_line(0, y, 1)
    ag_line(1, y, 1)
    pair_add(0, 1)
    line_edge(1, y1)
    prepare(1)
    partial(1, 0)
    pair_send(1, 0)
    ag_cross(1, 1)
    ag_line(0, y, 2)
    ag_line(1, y, 2)
    partial(1, 1)
    pair_send(1, 1)
    pair_add(1, 0)
    across_send(1)
    pair_add(1, 1)
    line_edge(1, y2)
    line_step(1, y1, 0)
    ag_cross(0, 0)
    for s in range(3, nd):
        ag_line(0, y, s)
        ag_line(1, y, s)
    for s in range(2, nd):
        ag_cross(1, s)
    pl.when(first)(across_add)
    line_edge(0, y, first)
    line_step(1, y1, 1)
    line_step(0, y, 0, first)
    line_step(1, y2, 0)
    for s in range(2, nd - 1):
        line_step(1, y1, s)
    line_end(1, y1)
    send(second, last_copy)
    line_step(0, y, 1, first)
    line_step(1, y2, 1)
    pl.when(second)(across_add)
    line_edge(0, y, second)
    line_step(0, y, 0, second)
    for s in range(2, nd - 1):
        line_step(0, y, s, first)
    for s in range(2, nd - 1):
        line_step(1, y2, s)
    line_end(1, y2)
    send(first, last_copy)
    for s in range(1, nd - 1):
        line_step(0, y, s, second)

    for s in range(1, nd):
        ag_cross(0, s)
    for p in range(2):
        for yy in range(NY):
            for zz in range(nd):
                ag_wait(None, p, blk(yy, oc, zz))

    def turned_copies(i):
        at = pl.ds(pl.multiple_of(i * tile, tile), tile)
        return (
            pltpu.make_async_copy(th.at[at, :], ath_ref.at[at, :], t_sem.at[0, i]),
            pltpu.make_async_copy(tl.at[at, :], atl_ref.at[at, :], t_sem.at[1, i]),
        )

    def turn(i, carry):
        at = pl.ds(pl.multiple_of(i * tile, tile), tile)
        block = acts[:, :, at].reshape(2 * NY * nd * tb, tile)
        high, low = split(block.T)
        th[at, :] = high
        tl[at, :] = low
        for copy in turned_copies(i):
            copy.start()
        return carry

    lax.fori_loop(0, tiles, turn, 0)

    line_end(0, y)
    last_copy().wait_recv()
    part[me, :, cols(1)] += ry_b[...]
    out_ref[...] = part[me]

    for i in range(tiles):
        for copy in turned_copies(i):
            copy.wait()
    for cond, make in started:
        if cond is None:
            make().wait_send()
        else:
            pl.when(cond)(lambda make=make: make().wait_send())


def weight_kernel(ath_ref, atl_ref, gh_ref, gl_ref, out_ref):
    high, g_high = ath_ref[...], gh_ref[...]
    left = jnp.concatenate([high, atl_ref[...], high], axis=1)
    right = jnp.concatenate([g_high, g_high, gl_ref[...]], axis=0)
    out_ref[...] = jnp.dot(left, right, preferred_element_type=jnp.float32)


def shards(rows, nc, nd, activations, grad_output, up_weight):
    tb, dm = activations.shape
    trow, df = grad_output.shape
    tokens = trow * rows
    tile = max(128, dm // 8)
    f32, bf16 = jnp.float32, jnp.bfloat16
    cuts = (0, (dm // tile * 5 // 8) * tile, dm)
    wa, wb = cuts[1], dm - cuts[1]
    vmem = pl.BlockSpec(memory_space=pltpu.VMEM)
    hbm = pl.BlockSpec(memory_space=pl.ANY)
    dma = pltpu.SemaphoreType.DMA
    grad_input, ath, atl, gh, gl = pl.pallas_call(
        functools.partial(exchange_kernel, rows, nd, cuts, tile),
        out_shape=(
            jax.ShapeDtypeStruct((tb, dm), f32),
            jax.ShapeDtypeStruct((dm, tokens), bf16),
            jax.ShapeDtypeStruct((dm, tokens), bf16),
            jax.ShapeDtypeStruct((tokens, df), bf16),
            jax.ShapeDtypeStruct((tokens, df), bf16),
        ),
        in_specs=[vmem, vmem, hbm],
        out_specs=(vmem, hbm, hbm, vmem, vmem),
        scratch_shapes=[
            pltpu.VMEM((nc * nd, tb, dm), f32),
            pltpu.VMEM((rows, trow, df), f32),
            pltpu.VMEM((NY, 2 * tokens // NY, df), bf16),
            pltpu.VMEM((dm, tokens), bf16),
            pltpu.VMEM((dm, tokens), bf16),
            pltpu.VMEM((min(3, dm // tile), tile, df), f32),
            pltpu.VMEM((dm, df), bf16),
            pltpu.VMEM((dm, df), bf16),
            pltpu.VMEM((nc * nd, tb, dm), f32),
            pltpu.VMEM((NY, nd, tb, dm), f32),
            pltpu.VMEM((nd, tb, wa), f32),
            pltpu.VMEM((tb, wb), f32),
            pltpu.VMEM((2, nd, tb, wa), f32),
            pltpu.VMEM((NY, 2, nd, tb, wb), f32),
            dma((2, dm // tile)),
            dma((3,)),
            dma((rows,)),
            dma((rows,)),
            dma((2, nc * nd, 4)),
            dma((2, nc * nd)),
            dma((NY, 2)),
            dma((NY, 2)),
            dma((nd,)),
            dma((nd,)),
            dma,
            dma,
            dma((2, nd)),
            dma((2, nd)),
            dma((NY, 2, nd)),
            dma((NY, 2, nd)),
        ],
        compiler_params=pltpu.CompilerParams(
            collective_id=0, has_side_effects=True, vmem_limit_bytes=62 * 2**20
        ),
        cost_estimate=pl.CostEstimate(
            flops=6 * tokens * dm * df, bytes_accessed=4 * dm * df, transcendentals=0
        ),
        name="exchange",
    )(activations, grad_output, up_weight)

    grad_weight = pl.pallas_call(
        weight_kernel,
        grid=(dm // tile,),
        out_shape=jax.ShapeDtypeStruct((dm, df), f32),
        in_specs=[
            pl.BlockSpec((tile, tokens), lambda i: (i, 0)),
            pl.BlockSpec((tile, tokens), lambda i: (i, 0)),
            pl.BlockSpec((tokens, df), lambda i: (0, 0)),
            pl.BlockSpec((tokens, df), lambda i: (0, 0)),
        ],
        out_specs=pl.BlockSpec((tile, df), lambda i: (i, 0)),
        compiler_params=pltpu.CompilerParams(vmem_limit_bytes=63 * 2**20),
        cost_estimate=pl.CostEstimate(
            flops=6 * tokens * dm * df, bytes_accessed=4 * dm * df, transcendentals=0
        ),
        name="weight_grad",
    )(ath, atl, gh, gl)
    return grad_input, grad_weight


def solution(mesh):
    rows, nc, nd = (mesh.shape[name] for name in ("row", "col", "depth"))
    return jax.shard_map(
        functools.partial(shards, rows, nc, nd),
        mesh=mesh,
        in_specs=(
            P(("col", "depth"), "row"),
            P("row", ("col", "depth")),
            P("row", ("col", "depth")),
        ),
        out_specs=(P(("col", "depth"), "row"), P("row", ("col", "depth"))),
        check_vma=False,
    )
```

```python
import functools

import jax
import jax.numpy as jnp
from jax import lax
from jax.experimental import pallas as pl
from jax.experimental.pallas import tpu as pltpu
from jax.sharding import PartitionSpec as P

MESH = pl.DeviceIdType.MESH
NY = 2
UP, DOWN, ACROSS, PAIR = range(4)


def both(a, b):
    return jnp.logical_and(a, b)


def split(value):
    high = value.astype(jnp.bfloat16)
    low = (value - high.astype(jnp.float32)).astype(jnp.bfloat16)
    return high, low


def dot_nt(a, b):
    return lax.dot_general(
        a, b, (((1,), (1,)), ((), ())), preferred_element_type=jnp.float32
    )


def exchange_kernel(
    rows, nd, cuts, tile,
    acts_ref, grads_ref, weight_ref,
    out_ref, left_ref, right_ref,
    acts, grads, turned, stage, wh, wl, part, rc, ry_a, ry_b, rz_a, rz_b,
    t_sem, w_sem, x_s, x_r, ag_s, ag_r, c_s, c_r, ya_s, ya_r, yb_s, yb_r, za_s, za_r, zb_s, zb_r,
):
    x = lax.axis_index("row")
    col = lax.axis_index("col")
    z = lax.axis_index("depth")
    y, c = col // 2, col % 2
    oy, oc = 1 - y, 1 - c
    y1 = x * NY // rows
    tb, dm = acts_ref.shape
    trow = grads_ref.shape[0]
    tiles = dm // tile
    per = rows // NY
    has_up, has_down = z < nd - 1, z > 0

    mate = {"col": 2 * y + oc}
    across = {"col": 2 * oy + c}
    above, below = {"depth": z + 1}, {"depth": z - 1}

    def blk(yy, cc, zz):
        return (2 * yy + cc) * nd + zz

    me = blk(y, c, z)
    started = []

    def send(cond, make):
        def go():
            make().start()

        started.append((cond, make))
        if cond is None:
            go()
        else:
            pl.when(cond)(go)

    def weight_copy(i, slot):
        return pltpu.make_async_copy(
            weight_ref.at[pl.ds(i * tile, tile), :], stage.at[slot], w_sem.at[slot]
        )

    slots = min(3, tiles)
    for i in range(slots):
        weight_copy(i, i).start()

    acts[me] = acts_ref[...]
    grads[x] = grads_ref[...]

    barrier = pltpu.get_barrier_semaphore()
    peers = [{"row": (x + d) % rows} for d in range(1, rows)]
    for peer in [mate, across] + peers:
        pl.semaphore_signal(barrier, inc=1, device_id=peer, device_id_type=MESH)

    @pl.when(has_up)
    def _():
        pl.semaphore_signal(barrier, inc=1, device_id=above, device_id_type=MESH)

    @pl.when(has_down)
    def _():
        pl.semaphore_signal(barrier, inc=1, device_id=below, device_id_type=MESH)

    lines = has_up.astype(jnp.int32) + has_down.astype(jnp.int32)
    pl.semaphore_wait(barrier, 2 + len(peers) + lines)

    def x_copy(d):
        return pltpu.make_async_remote_copy(
            src_ref=grads.at[x], dst_ref=grads.at[x],
            send_sem=x_s.at[d], recv_sem=x_r.at[x],
            device_id={"row": (x + d) % rows}, device_id_type=MESH,
        )

    for d in range(1, rows):
        send(None, functools.partial(x_copy, d))

    targets = {UP: above, DOWN: below, ACROSS: across, PAIR: mate}

    def ag_copy(p, b, way):
        ref = acts.at[b, :, pl.ds(cuts[p], cuts[p + 1] - cuts[p])]
        return pltpu.make_async_remote_copy(
            src_ref=ref, dst_ref=ref,
            send_sem=ag_s.at[p, b, way], recv_sem=ag_r.at[p, b],
            device_id=targets[way], device_id_type=MESH,
        )

    def ag_send(cond, p, b, way):
        send(cond, lambda: ag_copy(p, b, way))

    def ag_wait(cond, p, b):
        def go():
            ag_copy(p, b, PAIR).wait_recv()

        if cond is None:
            go()
        else:
            pl.when(cond)(go)

    for p in range(2):
        ag_send(has_up, p, me, UP)
        ag_send(has_down, p, me, DOWN)
    ag_send(None, 1, me, ACROSS)
    ag_send(None, 0, me, ACROSS)
    for p in range(2):
        ag_send(None, p, me, PAIR)

    def ag_line(p, yy, s):
        low, high = z - s >= 0, z + s <= nd - 1
        b_low, b_high = blk(yy, c, z - s), blk(yy, c, z + s)
        ag_wait(low, p, b_low)
        ag_send(both(low, has_up), p, b_low, UP)
        if p == 0:
            ag_send(low, p, b_low, ACROSS)
        ag_send(low, p, b_low, PAIR)
        ag_wait(high, p, b_high)
        ag_send(both(high, has_down), p, b_high, DOWN)
        if p == 0:
            ag_send(high, p, b_high, ACROSS)
        ag_send(high, p, b_high, PAIR)

    def ag_cross(p, s):
        if s == 0:
            b = blk(oy, c, z)
            ag_wait(None, p, b)
            if p == 1:
                ag_send(has_up, p, b, UP)
                ag_send(has_down, p, b, DOWN)
            ag_send(None, p, b, PAIR)
        elif p == 1:
            ag_line(1, oy, s)
        else:
            for cond, b in (
                (z - s >= 0, blk(oy, c, z - s)),
                (z + s <= nd - 1, blk(oy, c, z + s)),
            ):
                ag_wait(cond, 0, b)
                ag_send(cond, 0, b, PAIR)

    half = per * trow

    def prepare(phase):
        yy = (y1 + phase) % NY
        for j in range(per):
            q = yy * per + j

            @pl.when(q != x)
            def _():
                pltpu.make_async_remote_copy(
                    src_ref=grads.at[q], dst_ref=grads.at[q],
                    send_sem=x_s.at[0], recv_sem=x_r.at[q],
                    device_id=mate, device_id_type=MESH,
                ).wait_recv()

            high, low = split(grads[q])
            at = pl.multiple_of(yy * 2 * half + j * trow, trow)
            right_ref[pl.ds(at, trow), :] = high
            right_ref[pl.ds(pl.multiple_of(at + half, trow), trow), :] = low
            extra = pl.multiple_of(2 * NY * half + q * trow, trow)
            right_ref[pl.ds(extra, trow), :] = high

    def partial(phase, p):
        yy = (y1 + phase) % NY

        def step(i, carry):
            rows_at = pl.ds(pl.multiple_of(i * tile, tile), tile)
            if phase == 0:
                slot = i % slots
                weight_copy(i, slot).wait()
                high, low = split(stage[slot])
                wh[rows_at, :] = high
                wl[rows_at, :] = low

                @pl.when(i + slots < tiles)
                def _():
                    weight_copy(i + slots, slot).start()
            else:
                high, low = wh[rows_at, :], wl[rows_at, :]
            at = pl.multiple_of(yy * 2 * half, half)
            pairs = dot_nt(right_ref[pl.ds(at, 2 * half), :], high)
            crossed = dot_nt(right_ref[pl.ds(at, half), :], low)
            total = pairs[:half] + (pairs[half:] + crossed)
            part[pl.ds(yy * 2 * nd, 2 * nd), :, rows_at] = total.reshape(
                2 * nd, tb, tile
            )
            return carry

        lax.fori_loop(cuts[p] // tile, cuts[p + 1] // tile, step, 0)

    def cols(p):
        return pl.ds(cuts[p], cuts[p + 1] - cuts[p])

    def pair_copy(yy, p):
        return pltpu.make_async_remote_copy(
            src_ref=part.at[pl.ds(blk(yy, oc, 0), nd), :, cols(p)],
            dst_ref=rc.at[yy, :, :, cols(p)],
            send_sem=c_s.at[yy, p], recv_sem=c_r.at[yy, p],
            device_id=mate, device_id_type=MESH,
        )

    def pair_send(phase, p):
        yy = (y1 + phase) % NY
        send(None, functools.partial(pair_copy, yy, p))

    def pair_add(phase, p):
        yy = (y1 + phase) % NY
        pair_copy(yy, p).wait_recv()
        own = pl.ds(blk(yy, c, 0), nd)
        part[own, :, cols(p)] += rc[yy, :, :, cols(p)]

    def across_copy(t):
        return pltpu.make_async_remote_copy(
            src_ref=part.at[blk(oy, c, t), :, cols(0)], dst_ref=ry_a.at[t],
            send_sem=ya_s.at[t], recv_sem=ya_r.at[t],
            device_id=across, device_id_type=MESH,
        )

    def across_send(phase):
        yy = (y1 + phase) % NY
        for zz in range(nd):

            @pl.when(both(yy != y, z == zz))
            def _(zz=zz):
                for t in sorted(range(nd), key=lambda t: -abs(t - zz)):
                    across_copy(t).start()

        for t in range(nd):
            started.append((yy != y, functools.partial(across_copy, t)))

    def across_take(t):
        across_copy(t).wait_recv()
        part[blk(y, c, t), :, cols(0)] += ry_a[t]

    def line_copy(p, yy, t, way):
        if p == 0:
            dst, ss, rs = rz_a.at[way, t], za_s.at[way, t], za_r.at[way, t]
        else:
            dst, ss, rs = rz_b.at[yy, way, t], zb_s.at[yy, way, t], zb_r.at[yy, way, t]
        return pltpu.make_async_remote_copy(
            src_ref=part.at[blk(yy, c, t), :, cols(p)], dst_ref=dst,
            send_sem=ss, recv_sem=rs,
            device_id=targets[way], device_id_type=MESH,
        )

    def line_take(p, yy, t, way):
        line_copy(p, yy, t, way).wait_recv()
        got = rz_a[way, t] if p == 0 else rz_b[yy, way, t]
        part[blk(yy, c, t), :, cols(p)] += got

    def line_edge(p, yy, cond=None):
        for on, way, order in (
            (z == 0, UP, range(nd - 1, 0, -1)),
            (z == nd - 1, DOWN, range(nd - 1)),
        ):
            on = on if cond is None else both(cond, on)
            for t in order:
                if p == 0:
                    pl.when(on)(functools.partial(across_take, t))
                send(on, functools.partial(line_copy, p, yy, t, way))

    def line_step(p, yy, s, cond=None):
        for t, way, mine, more in (
            (nd - 1 - s, UP, z < nd - 1 - s, has_down),
            (s, DOWN, z > s, has_up),
        ):
            on = both(mine, more) if cond is None else both(cond, both(mine, more))
            if p == 0:
                pl.when(on)(functools.partial(across_take, t))
            pl.when(on)(functools.partial(line_take, p, yy, t, way))
            send(on, functools.partial(line_copy, p, yy, t, way))

    def line_end(p, yy, cond=None):
        for way, more in ((UP, has_down), (DOWN, has_up)):
            on = more if cond is None else both(cond, more)
            pl.when(on)(functools.partial(line_take, p, yy, z, way))

    def last_copy():
        return pltpu.make_async_remote_copy(
            src_ref=part.at[blk(oy, c, z), :, cols(1)], dst_ref=ry_b,
            send_sem=yb_s, recv_sem=yb_r,
            device_id=across, device_id_type=MESH,
        )

    y2 = (y1 + 1) % NY
    first, second = y == y1, y != y1

    prepare(0)
    for p in range(2):
        partial(0, p)
        pair_send(0, p)
    pair_add(0, 0)
    across_send(0)
    ag_cross(1, 0)
    ag_line(0, y, 1)
    ag_line(1, y, 1)
    pair_add(0, 1)
    line_edge(1, y1)
    prepare(1)
    for p in range(2):
        partial(1, p)
        pair_send(1, p)
    pair_add(1, 0)
    across_send(1)
    ag_cross(1, 1)
    ag_line(0, y, 2)
    ag_line(1, y, 2)
    pair_add(1, 1)
    line_edge(1, y2)
    line_edge(0, y, first)
    line_step(1, y1, 0)
    line_step(0, y, 0, first)
    ag_cross(0, 0)
    for s in range(3, nd):
        ag_line(0, y, s)
        ag_line(1, y, s)
    for s in range(2, nd):
        ag_cross(1, s)
    line_step(1, y2, 0)
    line_edge(0, y, second)
    line_step(0, y, 0, second)
    for s in range(1, nd - 1):
        line_step(1, y1, s)
        line_step(0, y, s, first)
        if s == nd - 2:
            line_end(1, y1)
            send(second, last_copy)
        line_step(1, y2, s)
        line_step(0, y, s, second)
        if s == 1:
            ag_cross(0, 1)
    line_end(1, y2)
    send(first, last_copy)

    for s in range(2, nd):
        ag_cross(0, s)
    for p in range(2):
        for yy in range(NY):
            for zz in range(nd):
                ag_wait(None, p, blk(yy, oc, zz))

    def turned_copy(i):
        at = pl.ds(pl.multiple_of(i * tile, tile), tile)
        return pltpu.make_async_copy(turned.at[at, :], left_ref.at[at, :], t_sem.at[i])

    def turn(i, carry):
        at = pl.ds(pl.multiple_of(i * tile, tile), tile)
        block = acts[:, :, at].reshape(2 * NY * nd * tb, tile)
        high, low = split(block.T)
        for yy in range(NY):
            own = high[:, yy * half : (yy + 1) * half]
            turned[at, 2 * yy * half : (2 * yy + 1) * half] = own
            turned[at, (2 * yy + 1) * half : (2 * yy + 2) * half] = own
        turned[at, 2 * NY * half :] = low
        turned_copy(i).start()
        return carry

    lax.fori_loop(0, tiles, turn, 0)

    across_take(z)
    line_end(0, y)
    last_copy().wait_recv()
    part[me, :, cols(1)] += ry_b[...]
    out_ref[...] = part[me]

    for i in range(tiles):
        turned_copy(i).wait()
    for cond, make in started:
        if cond is None:
            make().wait_send()
        else:
            pl.when(cond)(lambda make=make: make().wait_send())


def weight_kernel(left_ref, right_ref, out_ref):
    out_ref[...] = jnp.dot(
        left_ref[...], right_ref[...], preferred_element_type=jnp.float32
    )


def shards(rows, nc, nd, activations, grad_output, up_weight):
    tb, dm = activations.shape
    trow, df = grad_output.shape
    tokens = trow * rows
    tile = max(128, dm // 8)
    f32, bf16 = jnp.float32, jnp.bfloat16
    cuts = (0, (dm // tile * 5 // 8) * tile, dm)
    wa, wb = cuts[1], dm - cuts[1]
    vmem = pl.BlockSpec(memory_space=pltpu.VMEM)
    hbm = pl.BlockSpec(memory_space=pl.ANY)
    dma = pltpu.SemaphoreType.DMA
    grad_input, left, right = pl.pallas_call(
        functools.partial(exchange_kernel, rows, nd, cuts, tile),
        out_shape=(
            jax.ShapeDtypeStruct((tb, dm), f32),
            jax.ShapeDtypeStruct((dm, 3 * tokens), bf16),
            jax.ShapeDtypeStruct((3 * tokens, df), bf16),
        ),
        in_specs=[vmem, vmem, hbm],
        out_specs=(vmem, hbm, vmem),
        scratch_shapes=[
            pltpu.VMEM((nc * nd, tb, dm), f32),
            pltpu.VMEM((rows, trow, df), f32),
            pltpu.VMEM((dm, 3 * tokens), bf16),
            pltpu.VMEM((min(3, dm // tile), tile, df), f32),
            pltpu.VMEM((dm, df), bf16),
            pltpu.VMEM((dm, df), bf16),
            pltpu.VMEM((nc * nd, tb, dm), f32),
            pltpu.VMEM((NY, nd, tb, dm), f32),
            pltpu.VMEM((nd, tb, wa), f32),
            pltpu.VMEM((tb, wb), f32),
            pltpu.VMEM((2, nd, tb, wa), f32),
            pltpu.VMEM((NY, 2, nd, tb, wb), f32),
            dma((dm // tile,)),
            dma((3,)),
            dma((rows,)),
            dma((rows,)),
            dma((2, nc * nd, 4)),
            dma((2, nc * nd)),
            dma((NY, 2)),
            dma((NY, 2)),
            dma((nd,)),
            dma((nd,)),
            dma,
            dma,
            dma((2, nd)),
            dma((2, nd)),
            dma((NY, 2, nd)),
            dma((NY, 2, nd)),
        ],
        compiler_params=pltpu.CompilerParams(
            collective_id=0, has_side_effects=True, vmem_limit_bytes=62 * 2**20
        ),
        cost_estimate=pl.CostEstimate(
            flops=6 * tokens * dm * df, bytes_accessed=4 * dm * df, transcendentals=0
        ),
        name="exchange",
    )(activations, grad_output, up_weight)

    grad_weight = pl.pallas_call(
        weight_kernel,
        grid=(dm // tile,),
        out_shape=jax.ShapeDtypeStruct((dm, df), f32),
        in_specs=[
            pl.BlockSpec((tile, 3 * tokens), lambda i: (i, 0)),
            pl.BlockSpec((3 * tokens, df), lambda i: (0, 0)),
        ],
        out_specs=pl.BlockSpec((tile, df), lambda i: (i, 0)),
        compiler_params=pltpu.CompilerParams(vmem_limit_bytes=63 * 2**20),
        cost_estimate=pl.CostEstimate(
            flops=6 * tokens * dm * df, bytes_accessed=4 * dm * df, transcendentals=0
        ),
        name="weight_grad",
    )(left, right)
    return grad_input, grad_weight


def solution(mesh):
    rows, nc, nd = (mesh.shape[name] for name in ("row", "col", "depth"))
    return jax.shard_map(
        functools.partial(shards, rows, nc, nd),
        mesh=mesh,
        in_specs=(
            P(("col", "depth"), "row"),
            P("row", ("col", "depth")),
            P("row", ("col", "depth")),
        ),
        out_specs=(P(("col", "depth"), "row"), P("row", ("col", "depth"))),
        check_vma=False,
    )
```

```python
import functools

import jax
import jax.numpy as jnp
from jax import lax
from jax.experimental import pallas as pl
from jax.experimental.pallas import tpu as pltpu
from jax.sharding import PartitionSpec as P

MESH = pl.DeviceIdType.MESH
NY = 2
UP, DOWN, ACROSS, PAIR = range(4)


def both(a, b):
    return jnp.logical_and(a, b)


def split(value):
    high = value.astype(jnp.bfloat16)
    low = (value - high.astype(jnp.float32)).astype(jnp.bfloat16)
    return high, low


def dot_nt(a, b):
    return lax.dot_general(
        a, b, (((1,), (1,)), ((), ())), preferred_element_type=jnp.float32
    )


def exchange_kernel(
    rows, nd, cuts, tile,
    acts_ref, grads_ref, weight_ref,
    out_ref, feats_ref, grads_out_ref,
    acts, grads, gcat, stage, wh, wl, part, rc, ry_a, ry_b, rz_a, rz_b,
    t_sem, w_sem, x_s, x_r, ag_s, ag_r, c_s, c_r, ya_s, ya_r, yb_s, yb_r, za_s, za_r, zb_s, zb_r,
):
    x = lax.axis_index("row")
    col = lax.axis_index("col")
    z = lax.axis_index("depth")
    y, c = col // 2, col % 2
    oy, oc = 1 - y, 1 - c
    y1 = x * NY // rows
    tb, dm = acts_ref.shape
    trow = grads_ref.shape[0]
    tiles = dm // tile
    per = rows // NY
    has_up, has_down = z < nd - 1, z > 0

    mate = {"col": 2 * y + oc}
    across = {"col": 2 * oy + c}
    above, below = {"depth": z + 1}, {"depth": z - 1}

    def blk(yy, cc, zz):
        return (2 * yy + cc) * nd + zz

    me = blk(y, c, z)
    started = []

    def send(cond, make):
        def go():
            make().start()

        started.append((cond, make))
        if cond is None:
            go()
        else:
            pl.when(cond)(go)

    def weight_copy(i, slot):
        return pltpu.make_async_copy(
            weight_ref.at[pl.ds(i * tile, tile), :], stage.at[slot], w_sem.at[slot]
        )

    slots = min(3, tiles)
    for i in range(slots):
        weight_copy(i, i).start()

    acts[me] = acts_ref[...]
    grads[x] = grads_ref[...]

    barrier = pltpu.get_barrier_semaphore()
    peers = [{"row": (x + d) % rows} for d in range(1, rows)]
    for peer in [mate, across] + peers:
        pl.semaphore_signal(barrier, inc=1, device_id=peer, device_id_type=MESH)

    @pl.when(has_up)
    def _():
        pl.semaphore_signal(barrier, inc=1, device_id=above, device_id_type=MESH)

    @pl.when(has_down)
    def _():
        pl.semaphore_signal(barrier, inc=1, device_id=below, device_id_type=MESH)

    lines = has_up.astype(jnp.int32) + has_down.astype(jnp.int32)
    pl.semaphore_wait(barrier, 2 + len(peers) + lines)

    def x_copy(d):
        return pltpu.make_async_remote_copy(
            src_ref=grads.at[x], dst_ref=grads.at[x],
            send_sem=x_s.at[d], recv_sem=x_r.at[x],
            device_id={"row": (x + d) % rows}, device_id_type=MESH,
        )

    for d in range(1, rows):
        send(None, functools.partial(x_copy, d))

    targets = {UP: above, DOWN: below, ACROSS: across, PAIR: mate}

    def ag_copy(p, b, way):
        ref = acts.at[b, :, pl.ds(cuts[p], cuts[p + 1] - cuts[p])]
        return pltpu.make_async_remote_copy(
            src_ref=ref, dst_ref=ref,
            send_sem=ag_s.at[p, b, way], recv_sem=ag_r.at[p, b],
            device_id=targets[way], device_id_type=MESH,
        )

    def ag_send(cond, p, b, way):
        send(cond, lambda: ag_copy(p, b, way))

    def ag_wait(cond, p, b):
        def go():
            ag_copy(p, b, PAIR).wait_recv()

        if cond is None:
            go()
        else:
            pl.when(cond)(go)

    for p in range(2):
        ag_send(has_up, p, me, UP)
        ag_send(has_down, p, me, DOWN)
    ag_send(None, 1, me, ACROSS)
    ag_send(None, 0, me, ACROSS)
    for p in range(2):
        ag_send(None, p, me, PAIR)

    def ag_line(p, yy, s):
        low, high = z - s >= 0, z + s <= nd - 1
        b_low, b_high = blk(yy, c, z - s), blk(yy, c, z + s)
        ag_wait(low, p, b_low)
        ag_send(both(low, has_up), p, b_low, UP)
        if p == 0:
            ag_send(low, p, b_low, ACROSS)
        ag_send(low, p, b_low, PAIR)
        ag_wait(high, p, b_high)
        ag_send(both(high, has_down), p, b_high, DOWN)
        if p == 0:
            ag_send(high, p, b_high, ACROSS)
        ag_send(high, p, b_high, PAIR)

    def ag_cross(p, s):
        if s == 0:
            b = blk(oy, c, z)
            ag_wait(None, p, b)
            if p == 1:
                ag_send(has_up, p, b, UP)
                ag_send(has_down, p, b, DOWN)
            ag_send(None, p, b, PAIR)
        elif p == 1:
            ag_line(1, oy, s)
        else:
            for cond, b in (
                (z - s >= 0, blk(oy, c, z - s)),
                (z + s <= nd - 1, blk(oy, c, z + s)),
            ):
                ag_wait(cond, 0, b)
                ag_send(cond, 0, b, PAIR)

    half = per * trow

    def prepare(phase):
        yy = (y1 + phase) % NY
        for j in range(per):
            q = yy * per + j

            @pl.when(q != x)
            def _():
                pltpu.make_async_remote_copy(
                    src_ref=grads.at[q], dst_ref=grads.at[q],
                    send_sem=x_s.at[0], recv_sem=x_r.at[q],
                    device_id=mate, device_id_type=MESH,
                ).wait_recv()

            high, low = split(grads[q])
            gcat[phase, j * trow : (j + 1) * trow, :] = high
            gcat[phase, half + j * trow : half + (j + 1) * trow, :] = low

    def partial(phase, begin, end):
        yy = (y1 + phase) % NY

        def step(i, carry):
            rows_at = pl.ds(pl.multiple_of(i * tile, tile), tile)
            if phase == 0:
                slot = i % slots
                weight_copy(i, slot).wait()
                high, low = split(stage[slot])
                wh[rows_at, :] = high
                wl[rows_at, :] = low

                @pl.when(i + slots < tiles)
                def _():
                    weight_copy(i + slots, slot).start()
            else:
                high, low = wh[rows_at, :], wl[rows_at, :]
            pairs = dot_nt(gcat[phase], high)
            crossed = dot_nt(gcat[phase, :half, :], low)
            total = pairs[:half] + (pairs[half:] + crossed)
            part[pl.ds(yy * 2 * nd, 2 * nd), :, rows_at] = total.reshape(
                2 * nd, tb, tile
            )
            return carry

        lax.fori_loop(begin, end, step, 0)

    def cols(p):
        return pl.ds(cuts[p], cuts[p + 1] - cuts[p])

    def pair_copy(yy, p):
        return pltpu.make_async_remote_copy(
            src_ref=part.at[pl.ds(blk(yy, oc, 0), nd), :, cols(p)],
            dst_ref=rc.at[yy, :, :, cols(p)],
            send_sem=c_s.at[yy, p], recv_sem=c_r.at[yy, p],
            device_id=mate, device_id_type=MESH,
        )

    def pair_send(phase, p):
        yy = (y1 + phase) % NY
        send(None, functools.partial(pair_copy, yy, p))

    def pair_add(phase, p):
        yy = (y1 + phase) % NY
        pair_copy(yy, p).wait_recv()
        own = pl.ds(blk(yy, c, 0), nd)
        part[own, :, cols(p)] += rc[yy, :, :, cols(p)]

    def across_copy(t):
        return pltpu.make_async_remote_copy(
            src_ref=part.at[blk(oy, c, t), :, cols(0)], dst_ref=ry_a.at[t],
            send_sem=ya_s.at[t], recv_sem=ya_r.at[t],
            device_id=across, device_id_type=MESH,
        )

    def across_send(phase):
        yy = (y1 + phase) % NY
        for zz in range(nd):

            @pl.when(both(yy != y, z == zz))
            def _(zz=zz):
                for t in sorted(range(nd), key=lambda t: -abs(t - zz)):
                    across_copy(t).start()

        for t in range(nd):
            started.append((yy != y, functools.partial(across_copy, t)))

    def across_take(t):
        across_copy(t).wait_recv()
        part[blk(y, c, t), :, cols(0)] += ry_a[t]

    def line_copy(p, yy, t, way):
        if p == 0:
            dst, ss, rs = rz_a.at[way, t], za_s.at[way, t], za_r.at[way, t]
        else:
            dst, ss, rs = rz_b.at[yy, way, t], zb_s.at[yy, way, t], zb_r.at[yy, way, t]
        return pltpu.make_async_remote_copy(
            src_ref=part.at[blk(yy, c, t), :, cols(p)], dst_ref=dst,
            send_sem=ss, recv_sem=rs,
            device_id=targets[way], device_id_type=MESH,
        )

    def line_take(p, yy, t, way):
        line_copy(p, yy, t, way).wait_recv()
        got = rz_a[way, t] if p == 0 else rz_b[yy, way, t]
        part[blk(yy, c, t), :, cols(p)] += got

    def line_edge(p, yy, cond=None):
        for on, way, order in (
            (z == 0, UP, range(nd - 1, 0, -1)),
            (z == nd - 1, DOWN, range(nd - 1)),
        ):
            on = on if cond is None else both(cond, on)
            for t in order:
                if p == 0:
                    pl.when(on)(functools.partial(across_take, t))
                send(on, functools.partial(line_copy, p, yy, t, way))

    def line_step(p, yy, s, cond=None):
        for t, way, mine, more in (
            (nd - 1 - s, UP, z < nd - 1 - s, has_down),
            (s, DOWN, z > s, has_up),
        ):
            on = both(mine, more) if cond is None else both(cond, both(mine, more))
            if p == 0:
                pl.when(on)(functools.partial(across_take, t))
            pl.when(on)(functools.partial(line_take, p, yy, t, way))
            send(on, functools.partial(line_copy, p, yy, t, way))

    def line_end(p, yy, cond=None):
        for way, more in ((UP, has_down), (DOWN, has_up)):
            on = more if cond is None else both(cond, more)
            pl.when(on)(functools.partial(line_take, p, yy, z, way))

    def last_copy():
        return pltpu.make_async_remote_copy(
            src_ref=part.at[blk(oy, c, z), :, cols(1)], dst_ref=ry_b,
            send_sem=yb_s, recv_sem=yb_r,
            device_id=across, device_id_type=MESH,
        )

    y2 = (y1 + 1) % NY
    first, second = y == y1, y != y1

    def grads_copy():
        return pltpu.make_async_copy(grads, grads_out_ref, t_sem.at[0])

    def feats_copy():
        return pltpu.make_async_copy(acts, feats_ref, t_sem.at[1])

    middle = cuts[1] // tile
    some = (middle + 1) // 2
    prepare(0)
    partial(0, 0, middle)
    pair_send(0, 0)
    ag_cross(1, 0)
    ag_line(0, y, 1)
    ag_line(1, y, 1)
    pair_add(0, 0)
    across_send(0)
    partial(0, middle, tiles)
    pair_send(0, 1)
    prepare(1)
    grads_copy().start()
    partial(1, 0, some)
    ag_cross(1, 1)
    ag_line(0, y, 2)
    ag_line(1, y, 2)
    pair_add(0, 1)
    line_edge(1, y1)
    partial(1, some, middle)
    pair_send(1, 0)
    pair_add(1, 0)
    across_send(1)
    partial(1, middle, tiles)
    pair_send(1, 1)
    ag_cross(0, 0)
    for s in range(3, nd):
        ag_line(0, y, s)
        ag_line(1, y, s)
    pair_add(1, 1)
    line_edge(1, y2)
    line_edge(0, y, first)
    line_step(1, y1, 0)
    line_step(0, y, 0, first)
    for s in range(2, nd):
        ag_cross(1, s)
    line_step(1, y2, 0)
    line_edge(0, y, second)
    line_step(0, y, 0, second)
    for s in range(1, nd - 1):
        line_step(1, y1, s)
        line_step(0, y, s, first)
        if s == nd - 2:
            line_end(1, y1)
            send(second, last_copy)
        line_step(1, y2, s)
        line_step(0, y, s, second)
        if s == 1:
            ag_cross(0, 1)
    line_end(1, y2)
    send(first, last_copy)

    for s in range(2, nd):
        ag_cross(0, s)
    for p in range(2):
        for yy in range(NY):
            for zz in range(nd):
                ag_wait(None, p, blk(yy, oc, zz))

    feats_copy().start()

    across_take(z)
    line_end(0, y)
    last_copy().wait_recv()
    part[me, :, cols(1)] += ry_b[...]
    out_ref[...] = part[me]

    grads_copy().wait()
    feats_copy().wait()
    for cond, make in started:
        if cond is None:
            make().wait_send()
        else:
            pl.when(cond)(lambda make=make: make().wait_send())


def shards(rows, nc, nd, activations, grad_output, up_weight):
    tb, dm = activations.shape
    trow, df = grad_output.shape
    tokens = trow * rows
    tile = max(128, dm // 8)
    f32, bf16 = jnp.float32, jnp.bfloat16
    cuts = (0, (dm // tile * 5 // 8) * tile, dm)
    wa, wb = cuts[1], dm - cuts[1]
    vmem = pl.BlockSpec(memory_space=pltpu.VMEM)
    hbm = pl.BlockSpec(memory_space=pl.ANY)
    dma = pltpu.SemaphoreType.DMA
    grad_input, feats, grads = pl.pallas_call(
        functools.partial(exchange_kernel, rows, nd, cuts, tile),
        out_shape=(
            jax.ShapeDtypeStruct((tb, dm), f32),
            jax.ShapeDtypeStruct((nc * nd, tb, dm), f32),
            jax.ShapeDtypeStruct((rows, trow, df), f32),
        ),
        in_specs=[vmem, vmem, hbm],
        out_specs=(vmem, hbm, hbm),
        scratch_shapes=[
            pltpu.VMEM((nc * nd, tb, dm), f32),
            pltpu.VMEM((rows, trow, df), f32),
            pltpu.VMEM((NY, 2 * tokens // NY, df), bf16),
            pltpu.VMEM((min(3, dm // tile), tile, df), f32),
            pltpu.VMEM((dm, df), bf16),
            pltpu.VMEM((dm, df), bf16),
            pltpu.VMEM((nc * nd, tb, dm), f32),
            pltpu.VMEM((NY, nd, tb, dm), f32),
            pltpu.VMEM((nd, tb, wa), f32),
            pltpu.VMEM((tb, wb), f32),
            pltpu.VMEM((2, nd, tb, wa), f32),
            pltpu.VMEM((NY, 2, nd, tb, wb), f32),
            dma((2,)),
            dma((3,)),
            dma((rows,)),
            dma((rows,)),
            dma((2, nc * nd, 4)),
            dma((2, nc * nd)),
            dma((NY, 2)),
            dma((NY, 2)),
            dma((nd,)),
            dma((nd,)),
            dma,
            dma,
            dma((2, nd)),
            dma((2, nd)),
            dma((NY, 2, nd)),
            dma((NY, 2, nd)),
        ],
        compiler_params=pltpu.CompilerParams(
            collective_id=0, has_side_effects=True, vmem_limit_bytes=62 * 2**20
        ),
        cost_estimate=pl.CostEstimate(
            flops=6 * tokens * dm * df, bytes_accessed=4 * dm * df, transcendentals=0
        ),
        name="exchange",
    )(activations, grad_output, up_weight)

    grad_weight = lax.dot_general(
        feats.reshape(tokens, dm),
        grads.reshape(tokens, df),
        (((0,), (0,)), ((), ())),
        precision=lax.Precision.HIGH,
        preferred_element_type=f32,
    )
    return grad_input, grad_weight


def solution(mesh):
    rows, nc, nd = (mesh.shape[name] for name in ("row", "col", "depth"))
    return jax.shard_map(
        functools.partial(shards, rows, nc, nd),
        mesh=mesh,
        in_specs=(
            P(("col", "depth"), "row"),
            P("row", ("col", "depth")),
            P("row", ("col", "depth")),
        ),
        out_specs=(P(("col", "depth"), "row"), P("row", ("col", "depth"))),
        check_vma=False,
    )
```

```python
import functools

import jax
import jax.numpy as jnp
from jax import lax
from jax.experimental import pallas as pl
from jax.experimental.pallas import tpu as pltpu
from jax.sharding import PartitionSpec as P

MESH = pl.DeviceIdType.MESH
NY = 2
UP, DOWN, ACROSS, PAIR = range(4)


def both(a, b):
    return jnp.logical_and(a, b)


def split(value):
    high = value.astype(jnp.bfloat16)
    low = (value - high.astype(jnp.float32)).astype(jnp.bfloat16)
    return high, low


def dot_nt(a, b):
    return lax.dot_general(
        a, b, (((1,), (1,)), ((), ())), preferred_element_type=jnp.float32
    )


def exchange_kernel(
    rows, nd, cuts, tile,
    acts_ref, grads_ref, weight_ref,
    out_ref, feats_ref, grads_out_ref,
    acts, grads, gcat, stage, wh, wl, part, rc, ry_a, ry_b, rz_a, rz_b,
    t_sem, w_sem, x_s, x_r, ag_s, ag_r, c_s, c_r, ya_s, ya_r, yb_s, yb_r, za_s, za_r, zb_s, zb_r,
):
    x = lax.axis_index("row")
    col = lax.axis_index("col")
    z = lax.axis_index("depth")
    y, c = col // 2, col % 2
    oy, oc = 1 - y, 1 - c
    y1 = x * NY // rows
    tb, dm = acts_ref.shape
    trow = grads_ref.shape[0]
    tiles = dm // tile
    per = rows // NY
    has_up, has_down = z < nd - 1, z > 0

    mate = {"col": 2 * y + oc}
    across = {"col": 2 * oy + c}
    above, below = {"depth": z + 1}, {"depth": z - 1}

    def blk(yy, cc, zz):
        return (2 * yy + cc) * nd + zz

    me = blk(y, c, z)
    started = []

    def send(cond, make):
        def go():
            make().start()

        started.append((cond, make))
        if cond is None:
            go()
        else:
            pl.when(cond)(go)

    def weight_copy(i, slot):
        return pltpu.make_async_copy(
            weight_ref.at[pl.ds(i * tile, tile), :], stage.at[slot], w_sem.at[slot]
        )

    slots = min(3, tiles)
    for i in range(slots):
        weight_copy(i, i).start()

    acts[me] = acts_ref[...]
    grads[x] = grads_ref[...]

    barrier = pltpu.get_barrier_semaphore()
    peers = [{"row": (x + d) % rows} for d in range(1, rows)]
    for peer in [mate, across] + peers:
        pl.semaphore_signal(barrier, inc=1, device_id=peer, device_id_type=MESH)

    @pl.when(has_up)
    def _():
        pl.semaphore_signal(barrier, inc=1, device_id=above, device_id_type=MESH)

    @pl.when(has_down)
    def _():
        pl.semaphore_signal(barrier, inc=1, device_id=below, device_id_type=MESH)

    lines = has_up.astype(jnp.int32) + has_down.astype(jnp.int32)
    pl.semaphore_wait(barrier, 2 + len(peers) + lines)

    def x_copy(d):
        return pltpu.make_async_remote_copy(
            src_ref=grads.at[x], dst_ref=grads.at[x],
            send_sem=x_s.at[d], recv_sem=x_r.at[x],
            device_id={"row": (x + d) % rows}, device_id_type=MESH,
        )

    for d in range(1, rows):
        send(None, functools.partial(x_copy, d))

    targets = {UP: above, DOWN: below, ACROSS: across, PAIR: mate}

    def ag_copy(p, b, way):
        ref = acts.at[b, :, pl.ds(cuts[p], cuts[p + 1] - cuts[p])]
        return pltpu.make_async_remote_copy(
            src_ref=ref, dst_ref=ref,
            send_sem=ag_s.at[p, b, way], recv_sem=ag_r.at[p, b],
            device_id=targets[way], device_id_type=MESH,
        )

    def ag_send(cond, p, b, way):
        send(cond, lambda: ag_copy(p, b, way))

    def ag_wait(cond, p, b):
        def go():
            ag_copy(p, b, PAIR).wait_recv()

        if cond is None:
            go()
        else:
            pl.when(cond)(go)

    for p in range(2):
        ag_send(has_up, p, me, UP)
        ag_send(has_down, p, me, DOWN)
    ag_send(None, 1, me, ACROSS)
    ag_send(None, 0, me, ACROSS)
    for p in range(2):
        ag_send(None, p, me, PAIR)

    def ag_line(p, yy, s):
        low, high = z - s >= 0, z + s <= nd - 1
        b_low, b_high = blk(yy, c, z - s), blk(yy, c, z + s)
        ag_wait(low, p, b_low)
        ag_send(both(low, has_up), p, b_low, UP)
        if p == 0:
            ag_send(low, p, b_low, ACROSS)
        ag_send(low, p, b_low, PAIR)
        ag_wait(high, p, b_high)
        ag_send(both(high, has_down), p, b_high, DOWN)
        if p == 0:
            ag_send(high, p, b_high, ACROSS)
        ag_send(high, p, b_high, PAIR)

    def ag_cross(p, s):
        if s == 0:
            b = blk(oy, c, z)
            ag_wait(None, p, b)
            if p == 1:
                ag_send(has_up, p, b, UP)
                ag_send(has_down, p, b, DOWN)
            ag_send(None, p, b, PAIR)
        elif p == 1:
            ag_line(1, oy, s)
        else:
            for cond, b in (
                (z - s >= 0, blk(oy, c, z - s)),
                (z + s <= nd - 1, blk(oy, c, z + s)),
            ):
                ag_wait(cond, 0, b)
                ag_send(cond, 0, b, PAIR)

    half = per * trow

    def prepare(phase):
        yy = (y1 + phase) % NY
        for j in range(per):
            q = yy * per + j

            @pl.when(q != x)
            def _():
                pltpu.make_async_remote_copy(
                    src_ref=grads.at[q], dst_ref=grads.at[q],
                    send_sem=x_s.at[0], recv_sem=x_r.at[q],
                    device_id=mate, device_id_type=MESH,
                ).wait_recv()

            high, low = split(grads[q])
            gcat[phase, j * trow : (j + 1) * trow, :] = high
            gcat[phase, half + j * trow : half + (j + 1) * trow, :] = low

    def partial(phase, begin, end):
        yy = (y1 + phase) % NY

        def step(i, carry):
            rows_at = pl.ds(pl.multiple_of(i * tile, tile), tile)
            if phase == 0:
                slot = i % slots
                weight_copy(i, slot).wait()
                high, low = split(stage[slot])
                wh[rows_at, :] = high
                wl[rows_at, :] = low

                @pl.when(i + slots < tiles)
                def _():
                    weight_copy(i + slots, slot).start()
            else:
                high, low = wh[rows_at, :], wl[rows_at, :]
            pairs = dot_nt(gcat[phase], high)
            crossed = dot_nt(gcat[phase, :half, :], low)
            total = pairs[:half] + (pairs[half:] + crossed)
            part[pl.ds(yy * 2 * nd, 2 * nd), :, rows_at] = total.reshape(
                2 * nd, tb, tile
            )
            return carry

        lax.fori_loop(begin, end, step, 0)

    def cols(p):
        return pl.ds(cuts[p], cuts[p + 1] - cuts[p])

    def pair_copy(yy, p):
        return pltpu.make_async_remote_copy(
            src_ref=part.at[pl.ds(blk(yy, oc, 0), nd), :, cols(p)],
            dst_ref=rc.at[yy, :, :, cols(p)],
            send_sem=c_s.at[yy, p], recv_sem=c_r.at[yy, p],
            device_id=mate, device_id_type=MESH,
        )

    def pair_send(phase, p):
        yy = (y1 + phase) % NY
        send(None, functools.partial(pair_copy, yy, p))

    def pair_add(phase, p):
        yy = (y1 + phase) % NY
        pair_copy(yy, p).wait_recv()
        own = pl.ds(blk(yy, c, 0), nd)
        part[own, :, cols(p)] += rc[yy, :, :, cols(p)]

    def across_copy(t):
        return pltpu.make_async_remote_copy(
            src_ref=part.at[blk(oy, c, t), :, cols(0)], dst_ref=ry_a.at[t],
            send_sem=ya_s.at[t], recv_sem=ya_r.at[t],
            device_id=across, device_id_type=MESH,
        )

    def across_send(phase):
        yy = (y1 + phase) % NY
        for zz in range(nd):

            @pl.when(both(yy != y, z == zz))
            def _(zz=zz):
                for t in sorted(range(nd), key=lambda t: -abs(t - zz)):
                    across_copy(t).start()

        for t in range(nd):
            started.append((yy != y, functools.partial(across_copy, t)))

    def across_take(t):
        across_copy(t).wait_recv()
        part[blk(y, c, t), :, cols(0)] += ry_a[t]

    def line_copy(p, yy, t, way):
        if p == 0:
            dst, ss, rs = rz_a.at[way, t], za_s.at[way, t], za_r.at[way, t]
        else:
            dst, ss, rs = rz_b.at[yy, way, t], zb_s.at[yy, way, t], zb_r.at[yy, way, t]
        return pltpu.make_async_remote_copy(
            src_ref=part.at[blk(yy, c, t), :, cols(p)], dst_ref=dst,
            send_sem=ss, recv_sem=rs,
            device_id=targets[way], device_id_type=MESH,
        )

    def line_take(p, yy, t, way):
        line_copy(p, yy, t, way).wait_recv()
        got = rz_a[way, t] if p == 0 else rz_b[yy, way, t]
        part[blk(yy, c, t), :, cols(p)] += got

    def line_edge(p, yy, cond=None):
        for on, way, order in (
            (z == 0, UP, range(nd - 1, 0, -1)),
            (z == nd - 1, DOWN, range(nd - 1)),
        ):
            on = on if cond is None else both(cond, on)
            for t in order:
                if p == 0:
                    pl.when(on)(functools.partial(across_take, t))
                send(on, functools.partial(line_copy, p, yy, t, way))

    def line_step(p, yy, s, cond=None):
        for t, way, mine, more in (
            (nd - 1 - s, UP, z < nd - 1 - s, has_down),
            (s, DOWN, z > s, has_up),
        ):
            on = both(mine, more) if cond is None else both(cond, both(mine, more))
            if p == 0:
                pl.when(on)(functools.partial(across_take, t))
            pl.when(on)(functools.partial(line_take, p, yy, t, way))
            send(on, functools.partial(line_copy, p, yy, t, way))

    def line_end(p, yy, cond=None):
        for way, more in ((UP, has_down), (DOWN, has_up)):
            on = more if cond is None else both(cond, more)
            pl.when(on)(functools.partial(line_take, p, yy, z, way))

    def last_copy():
        return pltpu.make_async_remote_copy(
            src_ref=part.at[blk(oy, c, z), :, cols(1)], dst_ref=ry_b,
            send_sem=yb_s, recv_sem=yb_r,
            device_id=across, device_id_type=MESH,
        )

    y2 = (y1 + 1) % NY
    first, second = y == y1, y != y1

    def grads_copy():
        return pltpu.make_async_copy(grads, grads_out_ref, t_sem.at[0])

    def feats_copy():
        return pltpu.make_async_copy(acts, feats_ref, t_sem.at[1])

    middle = cuts[1] // tile
    some = (middle + 1) // 2
    prepare(0)
    partial(0, 0, middle)
    pair_send(0, 0)
    ag_cross(1, 0)
    ag_line(0, y, 1)
    ag_line(1, y, 1)
    pair_add(0, 0)
    across_send(0)
    partial(0, middle, tiles)
    pair_send(0, 1)
    prepare(1)
    grads_copy().start()
    pair_add(0, 1)
    line_edge(1, y1)
    partial(1, 0, some)
    ag_cross(1, 1)
    ag_line(0, y, 2)
    ag_line(1, y, 2)
    partial(1, some, middle)
    pair_send(1, 0)
    pair_add(1, 0)
    across_send(1)
    line_edge(0, y, first)
    line_step(1, y1, 0)
    for s in range(3, nd):
        ag_line(0, y, s)
        ag_line(1, y, s)
    partial(1, middle, tiles)
    pair_send(1, 1)
    line_step(0, y, 0, first)
    pair_add(1, 1)
    line_edge(1, y2)
    ag_cross(0, 0)
    for s in range(2, nd):
        ag_cross(1, s)
    line_step(1, y2, 0)
    line_edge(0, y, second)
    line_step(0, y, 0, second)
    for s in range(1, nd - 1):
        line_step(1, y1, s)
        line_step(0, y, s, first)
        if s == nd - 2:
            line_end(1, y1)
            send(second, last_copy)
        line_step(1, y2, s)
        line_step(0, y, s, second)
        if s == 1:
            ag_cross(0, 1)
    line_end(1, y2)
    send(first, last_copy)

    for s in range(2, nd):
        ag_cross(0, s)
    for p in range(2):
        for yy in range(NY):
            for zz in range(nd):
                ag_wait(None, p, blk(yy, oc, zz))

    feats_copy().start()

    across_take(z)
    line_end(0, y)
    last_copy().wait_recv()
    part[me, :, cols(1)] += ry_b[...]
    out_ref[...] = part[me]

    grads_copy().wait()
    feats_copy().wait()
    for cond, make in started:
        if cond is None:
            make().wait_send()
        else:
            pl.when(cond)(lambda make=make: make().wait_send())


def shards(rows, nc, nd, activations, grad_output, up_weight):
    tb, dm = activations.shape
    trow, df = grad_output.shape
    tokens = trow * rows
    tile = max(128, dm // 8)
    f32, bf16 = jnp.float32, jnp.bfloat16
    cuts = (0, (dm // tile * 5 // 8) * tile, dm)
    wa, wb = cuts[1], dm - cuts[1]
    vmem = pl.BlockSpec(memory_space=pltpu.VMEM)
    hbm = pl.BlockSpec(memory_space=pl.ANY)
    dma = pltpu.SemaphoreType.DMA
    grad_input, feats, grads = pl.pallas_call(
        functools.partial(exchange_kernel, rows, nd, cuts, tile),
        out_shape=(
            jax.ShapeDtypeStruct((tb, dm), f32),
            jax.ShapeDtypeStruct((nc * nd, tb, dm), f32),
            jax.ShapeDtypeStruct((rows, trow, df), f32),
        ),
        in_specs=[vmem, vmem, hbm],
        out_specs=(vmem, hbm, hbm),
        scratch_shapes=[
            pltpu.VMEM((nc * nd, tb, dm), f32),
            pltpu.VMEM((rows, trow, df), f32),
            pltpu.VMEM((NY, 2 * tokens // NY, df), bf16),
            pltpu.VMEM((min(3, dm // tile), tile, df), f32),
            pltpu.VMEM((dm, df), bf16),
            pltpu.VMEM((dm, df), bf16),
            pltpu.VMEM((nc * nd, tb, dm), f32),
            pltpu.VMEM((NY, nd, tb, dm), f32),
            pltpu.VMEM((nd, tb, wa), f32),
            pltpu.VMEM((tb, wb), f32),
            pltpu.VMEM((2, nd, tb, wa), f32),
            pltpu.VMEM((NY, 2, nd, tb, wb), f32),
            dma((2,)),
            dma((3,)),
            dma((rows,)),
            dma((rows,)),
            dma((2, nc * nd, 4)),
            dma((2, nc * nd)),
            dma((NY, 2)),
            dma((NY, 2)),
            dma((nd,)),
            dma((nd,)),
            dma,
            dma,
            dma((2, nd)),
            dma((2, nd)),
            dma((NY, 2, nd)),
            dma((NY, 2, nd)),
        ],
        compiler_params=pltpu.CompilerParams(
            collective_id=0, has_side_effects=True, vmem_limit_bytes=62 * 2**20
        ),
        cost_estimate=pl.CostEstimate(
            flops=6 * tokens * dm * df, bytes_accessed=4 * dm * df, transcendentals=0
        ),
        name="exchange",
    )(activations, grad_output, up_weight)

    grad_weight = lax.dot_general(
        feats.reshape(tokens, dm),
        grads.reshape(tokens, df),
        (((0,), (0,)), ((), ())),
        precision=lax.Precision.HIGH,
        preferred_element_type=f32,
    )
    return grad_input, grad_weight


def solution(mesh):
    rows, nc, nd = (mesh.shape[name] for name in ("row", "col", "depth"))
    return jax.shard_map(
        functools.partial(shards, rows, nc, nd),
        mesh=mesh,
        in_specs=(
            P(("col", "depth"), "row"),
            P("row", ("col", "depth")),
            P("row", ("col", "depth")),
        ),
        out_specs=(P(("col", "depth"), "row"), P("row", ("col", "depth"))),
        check_vma=False,
    )
```

```python
import functools

import jax
import jax.numpy as jnp
from jax import lax
from jax.experimental import pallas as pl
from jax.experimental.pallas import tpu as pltpu
from jax.sharding import PartitionSpec as P

MESH = pl.DeviceIdType.MESH
NY = 2
UP, DOWN, ACROSS, PAIR = range(4)


def both(a, b):
    return jnp.logical_and(a, b)


def split(value):
    high = value.astype(jnp.bfloat16)
    low = (value - high.astype(jnp.float32)).astype(jnp.bfloat16)
    return high, low


def dot_nt(a, b):
    return lax.dot_general(
        a, b, (((1,), (1,)), ((), ())), preferred_element_type=jnp.float32
    )


def exchange_kernel(
    rows, nd, cuts, tile,
    acts_ref, grads_ref, weight_ref,
    out_ref, feats_ref, grads_out_ref,
    acts, grads, gcat, stage, wh, wl, part, rc, ry_a, ry_b, rz_a, rz_b,
    t_sem, w_sem, x_s, x_r, ag_s, ag_r, c_s, c_r, ya_s, ya_r, yb_s, yb_r, za_s, za_r, zb_s, zb_r,
):
    x = lax.axis_index("row")
    col = lax.axis_index("col")
    z = lax.axis_index("depth")
    y, c = col // 2, col % 2
    oy, oc = 1 - y, 1 - c
    y1 = x * NY // rows
    tb, dm = acts_ref.shape
    trow = grads_ref.shape[0]
    tiles = dm // tile
    per = rows // NY
    has_up, has_down = z < nd - 1, z > 0

    mate = {"col": 2 * y + oc}
    across = {"col": 2 * oy + c}
    above, below = {"depth": z + 1}, {"depth": z - 1}

    def blk(yy, cc, zz):
        return (2 * yy + cc) * nd + zz

    me = blk(y, c, z)
    started = []

    def send(cond, make):
        def go():
            make().start()

        started.append((cond, make))
        if cond is None:
            go()
        else:
            pl.when(cond)(go)

    def weight_copy(i, slot):
        return pltpu.make_async_copy(
            weight_ref.at[pl.ds(i * tile, tile), :], stage.at[slot], w_sem.at[slot]
        )

    slots = min(3, tiles)
    for i in range(slots):
        weight_copy(i, i).start()

    acts[me] = acts_ref[...]
    grads[x] = grads_ref[...]

    barrier = pltpu.get_barrier_semaphore()
    peers = [{"row": (x + d) % rows} for d in range(1, rows)]
    for peer in [mate, across] + peers:
        pl.semaphore_signal(barrier, inc=1, device_id=peer, device_id_type=MESH)

    @pl.when(has_up)
    def _():
        pl.semaphore_signal(barrier, inc=1, device_id=above, device_id_type=MESH)

    @pl.when(has_down)
    def _():
        pl.semaphore_signal(barrier, inc=1, device_id=below, device_id_type=MESH)

    lines = has_up.astype(jnp.int32) + has_down.astype(jnp.int32)
    pl.semaphore_wait(barrier, 2 + len(peers) + lines)

    def x_copy(d):
        return pltpu.make_async_remote_copy(
            src_ref=grads.at[x], dst_ref=grads.at[x],
            send_sem=x_s.at[d], recv_sem=x_r.at[x],
            device_id={"row": (x + d) % rows}, device_id_type=MESH,
        )

    for d in range(1, rows):
        send(None, functools.partial(x_copy, d))

    targets = {UP: above, DOWN: below, ACROSS: across, PAIR: mate}

    def ag_copy(p, b, way):
        ref = acts.at[b, :, pl.ds(cuts[p], cuts[p + 1] - cuts[p])]
        return pltpu.make_async_remote_copy(
            src_ref=ref, dst_ref=ref,
            send_sem=ag_s.at[p, b, way], recv_sem=ag_r.at[p, b],
            device_id=targets[way], device_id_type=MESH,
        )

    def ag_send(cond, p, b, way):
        send(cond, lambda: ag_copy(p, b, way))

    def ag_wait(cond, p, b):
        def go():
            ag_copy(p, b, PAIR).wait_recv()

        if cond is None:
            go()
        else:
            pl.when(cond)(go)

    for p in range(2):
        ag_send(has_up, p, me, UP)
        ag_send(has_down, p, me, DOWN)
    ag_send(None, 1, me, ACROSS)
    ag_send(None, 0, me, ACROSS)
    for p in range(2):
        ag_send(None, p, me, PAIR)

    def ag_line(p, yy, s):
        low, high = z - s >= 0, z + s <= nd - 1
        b_low, b_high = blk(yy, c, z - s), blk(yy, c, z + s)
        ag_wait(low, p, b_low)
        ag_send(both(low, has_up), p, b_low, UP)
        if p == 0:
            ag_send(low, p, b_low, ACROSS)
        ag_send(low, p, b_low, PAIR)
        ag_wait(high, p, b_high)
        ag_send(both(high, has_down), p, b_high, DOWN)
        if p == 0:
            ag_send(high, p, b_high, ACROSS)
        ag_send(high, p, b_high, PAIR)

    def ag_cross(p, s):
        if s == 0:
            b = blk(oy, c, z)
            ag_wait(None, p, b)
            if p == 1:
                ag_send(has_up, p, b, UP)
                ag_send(has_down, p, b, DOWN)
            ag_send(None, p, b, PAIR)
        elif p == 1:
            ag_line(1, oy, s)
        else:
            for cond, b in (
                (z - s >= 0, blk(oy, c, z - s)),
                (z + s <= nd - 1, blk(oy, c, z + s)),
            ):
                ag_wait(cond, 0, b)
                ag_send(cond, 0, b, PAIR)

    half = per * trow

    def prepare(phase):
        yy = (y1 + phase) % NY
        for j in range(per):
            q = yy * per + j

            @pl.when(q != x)
            def _():
                pltpu.make_async_remote_copy(
                    src_ref=grads.at[q], dst_ref=grads.at[q],
                    send_sem=x_s.at[0], recv_sem=x_r.at[q],
                    device_id=mate, device_id_type=MESH,
                ).wait_recv()

            high, low = split(grads[q])
            gcat[phase, j * trow : (j + 1) * trow, :] = high
            gcat[phase, half + j * trow : half + (j + 1) * trow, :] = low

    def partial(phase, begin, end):
        yy = (y1 + phase) % NY

        def step(i, carry):
            rows_at = pl.ds(pl.multiple_of(i * tile, tile), tile)
            if phase == 0:
                slot = i % slots
                weight_copy(i, slot).wait()
                high, low = split(stage[slot])
                wh[rows_at, :] = high
                wl[rows_at, :] = low

                @pl.when(i + slots < tiles)
                def _():
                    weight_copy(i + slots, slot).start()
            else:
                high, low = wh[rows_at, :], wl[rows_at, :]
            pairs = dot_nt(gcat[phase], high)
            crossed = dot_nt(gcat[phase, :half, :], low)
            total = pairs[:half] + (pairs[half:] + crossed)
            part[pl.ds(yy * 2 * nd, 2 * nd), :, rows_at] = total.reshape(
                2 * nd, tb, tile
            )
            return carry

        lax.fori_loop(begin, end, step, 0)

    def cols(p):
        return pl.ds(cuts[p], cuts[p + 1] - cuts[p])

    def pair_copy(yy, p):
        return pltpu.make_async_remote_copy(
            src_ref=part.at[pl.ds(blk(yy, oc, 0), nd), :, cols(p)],
            dst_ref=rc.at[yy, :, :, cols(p)],
            send_sem=c_s.at[yy, p], recv_sem=c_r.at[yy, p],
            device_id=mate, device_id_type=MESH,
        )

    def pair_send(phase, p):
        yy = (y1 + phase) % NY
        send(None, functools.partial(pair_copy, yy, p))

    def pair_add(phase, p):
        yy = (y1 + phase) % NY
        pair_copy(yy, p).wait_recv()
        own = pl.ds(blk(yy, c, 0), nd)
        part[own, :, cols(p)] += rc[yy, :, :, cols(p)]

    def across_copy(t):
        return pltpu.make_async_remote_copy(
            src_ref=part.at[blk(oy, c, t), :, cols(0)], dst_ref=ry_a.at[t],
            send_sem=ya_s.at[t], recv_sem=ya_r.at[t],
            device_id=across, device_id_type=MESH,
        )

    def across_send(phase):
        yy = (y1 + phase) % NY
        for zz in range(nd):

            @pl.when(both(yy != y, z == zz))
            def _(zz=zz):
                for t in sorted(range(nd), key=lambda t: -abs(t - zz)):
                    across_copy(t).start()

        for t in range(nd):
            started.append((yy != y, functools.partial(across_copy, t)))

    def across_take(t):
        across_copy(t).wait_recv()
        part[blk(y, c, t), :, cols(0)] += ry_a[t]

    def line_copy(p, yy, t, way):
        if p == 0:
            dst, ss, rs = rz_a.at[way, t], za_s.at[way, t], za_r.at[way, t]
        else:
            dst, ss, rs = rz_b.at[yy, way, t], zb_s.at[yy, way, t], zb_r.at[yy, way, t]
        return pltpu.make_async_remote_copy(
            src_ref=part.at[blk(yy, c, t), :, cols(p)], dst_ref=dst,
            send_sem=ss, recv_sem=rs,
            device_id=targets[way], device_id_type=MESH,
        )

    def line_take(p, yy, t, way):
        line_copy(p, yy, t, way).wait_recv()
        got = rz_a[way, t] if p == 0 else rz_b[yy, way, t]
        part[blk(yy, c, t), :, cols(p)] += got

    def line_edge(p, yy, cond=None):
        for on, way, order in (
            (z == 0, UP, range(nd - 1, 0, -1)),
            (z == nd - 1, DOWN, range(nd - 1)),
        ):
            on = on if cond is None else both(cond, on)
            for t in order:
                if p == 0:
                    pl.when(on)(functools.partial(across_take, t))
                send(on, functools.partial(line_copy, p, yy, t, way))

    def line_step(p, yy, s, cond=None):
        for t, way, mine, more in (
            (nd - 1 - s, UP, z < nd - 1 - s, has_down),
            (s, DOWN, z > s, has_up),
        ):
            on = both(mine, more) if cond is None else both(cond, both(mine, more))
            if p == 0:
                pl.when(on)(functools.partial(across_take, t))
            pl.when(on)(functools.partial(line_take, p, yy, t, way))
            send(on, functools.partial(line_copy, p, yy, t, way))

    def line_end(p, yy, cond=None):
        for way, more in ((UP, has_down), (DOWN, has_up)):
            on = more if cond is None else both(cond, more)
            pl.when(on)(functools.partial(line_take, p, yy, z, way))

    def last_copy():
        return pltpu.make_async_remote_copy(
            src_ref=part.at[blk(oy, c, z), :, cols(1)], dst_ref=ry_b,
            send_sem=yb_s, recv_sem=yb_r,
            device_id=across, device_id_type=MESH,
        )

    y2 = (y1 + 1) % NY
    first, second = y == y1, y != y1

    def grads_copy():
        return pltpu.make_async_copy(grads, grads_out_ref, t_sem.at[0])

    def feats_copy():
        return pltpu.make_async_copy(acts, feats_ref, t_sem.at[1])

    middle = cuts[1] // tile
    some = (middle + 1) // 2
    prepare(0)
    partial(0, 0, middle)
    pair_send(0, 0)
    ag_cross(1, 0)
    ag_line(0, y, 1)
    ag_line(1, y, 1)
    pair_add(0, 0)
    across_send(0)
    partial(0, middle, tiles)
    pair_send(0, 1)
    prepare(1)
    grads_copy().start()
    pair_add(0, 1)
    line_edge(1, y1)
    partial(1, 0, some)
    ag_cross(1, 1)
    ag_line(0, y, 2)
    ag_line(1, y, 2)
    partial(1, some, middle)
    pair_send(1, 0)
    pair_add(1, 0)
    across_send(1)
    line_edge(0, y, first)
    line_step(1, y1, 0)
    for s in range(3, nd):
        ag_line(0, y, s)
        ag_line(1, y, s)
    partial(1, middle, tiles)
    pair_send(1, 1)
    line_step(0, y, 0, first)
    pair_add(1, 1)
    line_edge(1, y2)
    ag_cross(0, 0)
    for s in range(2, nd):
        ag_cross(1, s)
    line_step(1, y2, 0)
    line_edge(0, y, second)
    line_step(0, y, 0, second)
    for s in range(1, nd - 1):
        line_step(1, y1, s)
        line_step(0, y, s, first)
        if s == nd - 2:
            line_end(1, y1)
            send(second, last_copy)
        line_step(1, y2, s)
        line_step(0, y, s, second)
        if s == 1:
            ag_cross(0, 1)
    line_end(1, y2)
    send(first, last_copy)

    for s in range(2, nd):
        ag_cross(0, s)
    for p in range(2):
        for yy in range(NY):
            for zz in range(nd):
                ag_wait(None, p, blk(yy, oc, zz))

    feats_copy().start()

    across_take(z)
    line_end(0, y)
    last_copy().wait_recv()
    part[me, :, cols(1)] += ry_b[...]
    out_ref[...] = part[me]

    grads_copy().wait()
    feats_copy().wait()
    for cond, make in started:
        if cond is None:
            make().wait_send()
        else:
            pl.when(cond)(lambda make=make: make().wait_send())


def shards(rows, nc, nd, activations, grad_output, up_weight):
    tb, dm = activations.shape
    trow, df = grad_output.shape
    tokens = trow * rows
    tile = max(128, dm // 8)
    f32, bf16 = jnp.float32, jnp.bfloat16
    cuts = (0, (dm // tile * 4 // 8) * tile, dm)
    wa, wb = cuts[1], dm - cuts[1]
    vmem = pl.BlockSpec(memory_space=pltpu.VMEM)
    hbm = pl.BlockSpec(memory_space=pl.ANY)
    dma = pltpu.SemaphoreType.DMA
    grad_input, feats, grads = pl.pallas_call(
        functools.partial(exchange_kernel, rows, nd, cuts, tile),
        out_shape=(
            jax.ShapeDtypeStruct((tb, dm), f32),
            jax.ShapeDtypeStruct((nc * nd, tb, dm), f32),
            jax.ShapeDtypeStruct((rows, trow, df), f32),
        ),
        in_specs=[vmem, vmem, hbm],
        out_specs=(vmem, hbm, hbm),
        scratch_shapes=[
            pltpu.VMEM((nc * nd, tb, dm), f32),
            pltpu.VMEM((rows, trow, df), f32),
            pltpu.VMEM((NY, 2 * tokens // NY, df), bf16),
            pltpu.VMEM((min(3, dm // tile), tile, df), f32),
            pltpu.VMEM((dm, df), bf16),
            pltpu.VMEM((dm, df), bf16),
            pltpu.VMEM((nc * nd, tb, dm), f32),
            pltpu.VMEM((NY, nd, tb, dm), f32),
            pltpu.VMEM((nd, tb, wa), f32),
            pltpu.VMEM((tb, wb), f32),
            pltpu.VMEM((2, nd, tb, wa), f32),
            pltpu.VMEM((NY, 2, nd, tb, wb), f32),
            dma((2,)),
            dma((3,)),
            dma((rows,)),
            dma((rows,)),
            dma((2, nc * nd, 4)),
            dma((2, nc * nd)),
            dma((NY, 2)),
            dma((NY, 2)),
            dma((nd,)),
            dma((nd,)),
            dma,
            dma,
            dma((2, nd)),
            dma((2, nd)),
            dma((NY, 2, nd)),
            dma((NY, 2, nd)),
        ],
        compiler_params=pltpu.CompilerParams(
            collective_id=0, has_side_effects=True, vmem_limit_bytes=62 * 2**20
        ),
        cost_estimate=pl.CostEstimate(
            flops=6 * tokens * dm * df, bytes_accessed=4 * dm * df, transcendentals=0
        ),
        name="exchange",
    )(activations, grad_output, up_weight)

    grad_weight = lax.dot_general(
        feats.reshape(tokens, dm),
        grads.reshape(tokens, df),
        (((0,), (0,)), ((), ())),
        precision=lax.Precision.HIGH,
        preferred_element_type=f32,
    )
    return grad_input, grad_weight


def solution(mesh):
    rows, nc, nd = (mesh.shape[name] for name in ("row", "col", "depth"))
    return jax.shard_map(
        functools.partial(shards, rows, nc, nd),
        mesh=mesh,
        in_specs=(
            P(("col", "depth"), "row"),
            P("row", ("col", "depth")),
            P("row", ("col", "depth")),
        ),
        out_specs=(P(("col", "depth"), "row"), P("row", ("col", "depth"))),
        check_vma=False,
    )
```
